32 devices in a mesh: row: 8 (over z, core), col: 4 (over y, x).
Axes of the slice: x: 2, y: 2, z: 4, core: 2. Of those that a mesh axis runs over, the one named last changes fastest.
Arguments:
- tokens: bfloat16 [1024, 12288], P('col', 'row'), may hold values from -6 to 6
- weight: bfloat16 [12288, 24576], P('row', 'col'), may hold values from -0.0546875 to 0.0546875
- cotangent: bfloat16 [1024, 24576], P('row', 'col'), may hold values from -6 to 6
Outputs:
- activated: bfloat16 [1024, 24576], P('row', 'col')
- input_grad: bfloat16 [1024, 12288], P('col', 'row')
- weight_grad: bfloat16 [12288, 24576], P('row', 'col')
The draws below stay inside these ranges and needn't reach their ends.
All inputs are finite; a program needn't handle non-finite values.
Results may differ from the reference program's by a relative error of at most 0.03.
Values may be sent and summed in bfloat16 or wider, within the bound.
No kernel may reach another device: no remote copies, remote signals or barrier semaphores. Data moves between devices by JAX's collectives and lax.ppermute only.
A program may use at most 128 MiB of HBM per device.

```python
import math
import jax
import jax.numpy as jnp
from jax import lax

D = 12288
FF = 24576
TOKENS = 1024
N_ROW = 8
N_COL = 4


def levels(stream_key, extent, split, low, high):
    gain = 1.0
    for axis_at, parts in split:
        heights = jax.random.uniform(jax.random.fold_in(jax.random.fold_in(stream_key, 6), axis_at), (parts,), jnp.float32, low / len(split), high / len(split))
        gain = gain * jnp.repeat(jnp.exp(heights), extent[axis_at] // parts).reshape((-1,) + (1,) * (len(extent) - 1 - axis_at))
    return gain


def scatter_about(stream_key, shape, spread, bound, pieces=(), held_as=jnp.bfloat16):
    gain = levels(stream_key, shape, pieces, -0.22, 0.18) if pieces else 1.0
    array = jax.random.normal(stream_key, shape, jnp.float32) * spread * gain
    return jnp.minimum(jnp.maximum(array, -bound), bound).astype(held_as)


def setup_inputs(seed: int = 0) -> dict:
    splits = jax.random.split(jax.random.key(seed), 4)
    tokens = scatter_about(splits[0], (TOKENS, D), 1.0, 6.0, ((0, 4), (1, 8)))
    weight = scatter_about(splits[1], (D, FF), D ** -0.5, 0.0546875, ((0, 8), (1, 4)))
    cotangent = scatter_about(splits[2], (TOKENS, FF), 1.0, 6.0, ((0, 8), (1, 4)))
    return {"tokens": tokens, "weight": weight, "cotangent": cotangent}


def gelu_exact(value):
    return 0.5 * value * (1.0 + jax.scipy.special.erf(value / math.sqrt(2.0)))

def gelu_slope(value):
    return 0.5 * (1.0 + jax.scipy.special.erf(value / math.sqrt(2.0))) + value * jnp.exp(-0.5 * value * value) / math.sqrt(2.0 * math.pi)

def reference(tokens, weight, cotangent):
    width_block = D // N_ROW
    unit_block = FF // N_COL

    def forward_step(total, index):
        start = (index * width_block).astype(jnp.int32)
        left = lax.dynamic_slice_in_dim(tokens, start, width_block, 1)
        right = lax.dynamic_slice_in_dim(weight, start, width_block, 0)
        partial_sum = jnp.dot(left, right, preferred_element_type=jnp.float32)
        rounded = lax.optimization_barrier(partial_sum.astype(jnp.bfloat16))
        return (total + rounded.astype(jnp.float32), None)
    pre, _ = lax.scan(forward_step, jnp.zeros((TOKENS, FF), jnp.float32), jnp.arange(N_ROW, dtype=jnp.int32))
    activated = gelu_exact(pre).astype(jnp.bfloat16)
    slope_grad = (cotangent.astype(jnp.float32) * gelu_slope(pre)).astype(jnp.bfloat16)

    def back_step(total, index):
        start = (index * unit_block).astype(jnp.int32)
        left = lax.dynamic_slice_in_dim(slope_grad, start, unit_block, 1)
        right = lax.dynamic_slice_in_dim(weight, start, unit_block, 1)
        partial_sum = lax.dot_general(left, right, (((1,), (1,)), ((), ())), preferred_element_type=jnp.float32)
        rounded = lax.optimization_barrier(partial_sum.astype(jnp.bfloat16))
        return (total + rounded.astype(jnp.float32), None)
    back_total, _ = lax.scan(back_step, jnp.zeros((TOKENS, D), jnp.float32), jnp.arange(N_COL, dtype=jnp.int32))
    input_grad = back_total.astype(jnp.bfloat16)
    weight_grad = lax.dot_general(tokens, slope_grad, (((0,), (0,)), ((), ())), preferred_element_type=jnp.float32).astype(jnp.bfloat16)
    return (activated, input_grad, weight_grad)
```

```python
import math

import jax
import jax.numpy as jnp
from jax import lax
from jax.experimental import pallas as pl
from jax.experimental.pallas import tpu as pltpu
from jax.sharding import PartitionSpec as P

BF16 = jnp.bfloat16
F32 = jnp.float32
CORES = 2
CHUNKS = 4
STREAMS = 2
HALVES = 2


def gelu_exact(value):
    return 0.5 * value * (1.0 + jax.scipy.special.erf(value / math.sqrt(2.0)))


def gelu_slope(value):
    return 0.5 * (1.0 + jax.scipy.special.erf(value / math.sqrt(2.0))) + value * jnp.exp(
        -0.5 * value * value
    ) / math.sqrt(2.0 * math.pi)


def tile(extent, limit):
    best = 128
    for size in range(128, min(extent, limit) + 1, 128):
        if extent % size == 0:
            best = size
    return best


def weight_grad_chunk(lefts, rights, buffer, chunk, all_units):
    width, depth = lefts[0].shape
    units = rights[0].shape[1]
    bm, bn = tile(width, 768), tile(units, 512)
    steps = units // bn
    kept = [] if buffer is None else [buffer]
    n = len(lefts)

    def body(*refs):
        total = jnp.dot(refs[0][...], refs[n][...], preferred_element_type=F32)
        for i in range(1, n):
            total += jnp.dot(refs[i][...], refs[n + i][...], preferred_element_type=F32)
        refs[-1][...] = total.astype(BF16)

    return pl.pallas_call(
        body,
        grid=(width // bm, steps),
        in_specs=[pl.BlockSpec((bm, depth), lambda i, j: (i, 0))] * n
        + [pl.BlockSpec((depth, bn), lambda i, j: (0, j))] * n
        + [pl.BlockSpec(memory_space=pl.ANY)] * len(kept),
        out_specs=pl.BlockSpec((bm, bn), lambda i, j: (i, chunk * steps + j)),
        out_shape=jax.ShapeDtypeStruct((width, all_units), BF16),
        input_output_aliases={2 * n: 0} if kept else {},
        compiler_params=pltpu.CompilerParams(vmem_limit_bytes=24 * 2**20),
        cost_estimate=pl.CostEstimate(
            flops=2 * n * width * depth * units,
            bytes_accessed=2 * width * units + 4 * n * depth * units,
            transcendentals=0,
        ),
        name="weight_grad",
    )(*lefts, *rights, *kept)


def on_device(tokens, weight, cotangent):
    n_row, n_col = lax.axis_size("row"), lax.axis_size("col")
    depth = n_row // CORES
    row, col = lax.axis_index("row"), lax.axis_index("col")
    z, core = row // CORES, row % CORES
    width, units = weight.shape
    share = cotangent.shape[0]
    few = share // HALVES
    f = units // CHUNKS
    square = n_col == 4 and depth == 4

    swap = [(r, r ^ 1) for r in range(n_row)]

    def right(places):
        return [(p * CORES + c, (p + 1) * CORES + c) for p in places for c in range(CORES)]

    def left(places):
        return [(p * CORES + c, (p - 1) * CORES + c) for p in places for c in range(CORES)]

    def cross(value, offset):
        return lax.ppermute(value, "col", [(c, c ^ offset) for c in range(4)])

    env = {}

    def fence(*names):
        names = [n for n in names if n in env]
        for name, value in zip(names, lax.optimization_barrier([env[n] for n in names])):
            env[name] = value

    def gather(half):
        mine = tokens.reshape(-1, share, width)[:, half * few : (half + 1) * few]
        if square:
            by_x, by_y = cross(mine, 1), cross(mine, 2)
            far = jnp.stack([cross(by_x[0], 2), cross(by_y[1], 1)])
            held = jnp.stack([mine, by_x, by_y, far])
            order = [col ^ ((z + j) % depth) for j in range(depth)]
        else:
            held = lax.all_gather(mine, "col", axis=0, tiled=True)
            held = held.reshape(depth, CORES, few, width)
            order = [(z + j) % depth for j in range(depth)]
        for name, which in (("own", core), ("other", 1 - core)):
            env[name, half] = jnp.concatenate(
                [lax.dynamic_slice(held, (b, which, 0, 0), (1, 1, few, width))[0, 0] for b in order]
            )

    def rows_of(half):
        return slice(half * few, (half + 1) * few)

    def columns_of(chunk):
        return slice(chunk * f, (chunk + 1) * f)

    per_half = CHUNKS // STREAMS
    items = [
        [(half, n * STREAMS + q) for half in range(HALVES) for n in range(per_half)]
        for q in range(STREAMS)
    ]
    count = HALVES * per_half
    slots = [(i, t) for i in range(count) for t in range(depth)]
    slots += [(count, t) for t in range(depth - 2)]

    activated = {}
    done = []

    def forward_other(q, i):
        half, chunk = items[q][i]
        part = jnp.dot(env["other", half], weight[:, columns_of(chunk)], preferred_element_type=F32)
        env["swapped", q] = lax.ppermute(part.astype(BF16), "row", swap)

    def forward_own(q, i):
        half, chunk = items[q][i]
        part = jnp.dot(env["own", half], weight[:, columns_of(chunk)], preferred_element_type=F32)
        part = (part + env["swapped", q].astype(F32)).astype(BF16)
        env["part", q] = part.reshape(depth, few, f)
        done.append(("part", q))

    def backward_input(q, i):
        half, chunk = items[q][i]
        for name in ("own", "other"):
            grad = lax.dot_general(
                env[name + "_g", half, chunk],
                weight[:, columns_of(chunk)],
                (((1,), (1,)), ((), ())),
                preferred_element_type=F32,
            )
            key = (name + "_total", half)
            env[key] = env[key] + grad if key in env else grad
            done.append(key)

    def backward_weight(q, i):
        half, chunk = items[q][i]
        if half < HALVES - 1:
            return
        lefts, rights = [], []
        for h in range(HALVES):
            for name in ("own", "other"):
                lefts.append(env[name + "_t", h])
                rights.append(env[name + "_g", h, chunk])
        env["weight_grad"] = weight_grad_chunk(
            lefts, rights, env.get("weight_grad"), chunk, units
        )
        done.append("weight_grad")

    def scatter_input(half):
        own, other = env["own_total", half], env["other_total", half]
        pair = [
            jnp.where(core == c, own, other).astype(BF16).reshape(depth, 1, few, width)
            for c in range(CORES)
        ]
        pair = jnp.concatenate(pair, axis=1)
        if square:
            blocks = []
            for offset in range(4):
                at = ((col ^ offset) + depth - z) % depth
                block = lax.dynamic_slice(pair, (at, 0, 0, 0), (1, CORES, few, width))[0]
                blocks.append(cross(block, offset) if offset else block)
            total = sum(b.astype(F32) for b in blocks).astype(BF16)
        else:
            pair = lax.dynamic_slice(
                jnp.concatenate([pair, pair]), ((depth - z) % depth, 0, 0, 0), pair.shape
            )
            total = lax.psum_scatter(
                pair.reshape(n_col, -1, few, width), "col", scatter_dimension=0, tiled=True
            )[0]
        return total

    def finish(q, slot):
        i, t = slots[slot]
        key = ("recv", q)
        from_left, from_right = env[key, "r"], env[key, "l"]
        if t == depth - 2:
            half, chunk = items[q][i]
            pre = env["part", q][0].astype(F32) + from_left.astype(F32) + from_right.astype(F32)
            activated[half, chunk] = gelu_exact(pre).astype(BF16)
            slope = cotangent[rows_of(half), columns_of(chunk)].astype(F32) * gelu_slope(pre)
            env["slope", q] = slope.astype(BF16)
            return
        if t == depth - 1:
            i, step = i + 1, 1
        else:
            step = t + 2
        if i == 0:
            return
        env["got", q, step, "r"], env["got", q, step, "l"] = from_left, from_right
        if step == depth - 1:
            half, chunk = items[q][i - 1]
            blocks = [env["slope", q]]
            for j in range(1, depth):
                blocks.append(
                    jnp.where(
                        z + j < depth, env["got", q, j, "l"], env["got", q, depth - j, "r"]
                    )
                )
            env["own_g", half, chunk] = jnp.concatenate(blocks)
            env["other_g", half, chunk] = lax.ppermute(
                env["own_g", half, chunk], "row", swap
            )

    def message(q, slot):
        i, t = slots[slot]
        if t == depth - 1:
            env["msg", q, "r"] = env["msg", q, "l"] = env["slope", q]
            return
        for way, place, block in (("r", z, depth - 1 - t), ("l", depth - 1 - z, t + 1)):
            came = env.get((("recv", q), way))
            if i == count:
                value = came
            else:
                mine = env["part", q][block]
                if t == 0:
                    value = mine if i == 0 else jnp.where(place == 0, mine, came)
                else:
                    value = (came.astype(F32) + jnp.where(place <= t, mine, 0).astype(F32)).astype(BF16)
            env["msg", q, way] = value

    def start(q, slot):
        i, t = slots[slot]
        first = t + 1 if i == count else 0
        last = t + 1 if (i == 0 and t < depth - 2) else depth - 1
        places = range(first, last)
        env[("recv", q), "r"] = lax.ppermute(env["msg", q, "r"], "row", right(places))
        env[("recv", q), "l"] = lax.ppermute(
            env["msg", q, "l"], "row", left([depth - 1 - p for p in places])
        )

    def work(q, slot):
        i, t = slots[slot]
        pieces = []
        if t == depth - 2 and i < count:
            if i > 0:
                pieces.append((backward_input, i - 1))
            if i + 1 < count:
                pieces.append((forward_other, i + 1))
        if t == depth - 1 and i + 1 < count:
            pieces.append((forward_own, i + 1))
        if t == 0 and i > 1:
            pieces.append((backward_weight, i - 2))
        return pieces

    def reads(piece, q, i):
        half, chunk = items[q][i]
        if piece is forward_other:
            return [("other", half)]
        if piece is forward_own:
            return [("own", half)]
        return [("own_g", half, chunk)]

    gather(0)
    for q in range(STREAMS):
        forward_other(q, 0)
    for q in range(STREAMS):
        forward_own(q, 0)
        message(q, 0)
        start(q, 0)
    gather(1)
    for half in range(HALVES):
        for name in ("own", "other"):
            env[name + "_t", half] = env[name, half].T
    done.clear()
    input_grad = {}
    for slot in range(len(slots)):
        for q in range(STREAMS):
            fence((("recv", q), "r"), (("recv", q), "l"), *done)
            done.clear()
            finish(q, slot)
            if slot + 1 == len(slots):
                continue
            message(q, slot + 1)
            pieces = work(q, slot + 1)
            names = [n for piece, i in pieces for n in reads(piece, q, i)]
            fence(("msg", q, "r"), ("msg", q, "l"), *names)
            start(q, slot + 1)
            for piece, i in pieces:
                piece(q, i)
        i, t = slots[slot]
        if t == depth - 1 and i == per_half:
            for half in range(HALVES - 1):
                input_grad[half] = scatter_input(half)
    for q in range(STREAMS):
        backward_input(q, count - 1)
    input_grad[HALVES - 1] = scatter_input(HALVES - 1)
    for q in range(STREAMS):
        backward_weight(q, count - 1)

    halves = range(HALVES)
    activated = jnp.concatenate(
        [jnp.concatenate([activated[h, c] for c in range(CHUNKS)], axis=1) for h in halves]
    )
    input_grad = jnp.concatenate([input_grad[h] for h in halves], axis=-2)
    return activated, input_grad.reshape(tokens.shape), env["weight_grad"]


def solution(mesh):
    return jax.shard_map(
        on_device,
        mesh=mesh,
        in_specs=(P("col", "row"), P("row", "col"), P("row", "col")),
        out_specs=(P("row", "col"), P("col", "row"), P("row", "col")),
        check_vma=False,
    )
```

```python
import math

import jax
import jax.numpy as jnp
from jax import lax
from jax.experimental import pallas as pl
from jax.experimental.pallas import tpu as pltpu
from jax.sharding import PartitionSpec as P

BF16 = jnp.bfloat16
F32 = jnp.float32
CORES = 2
CHUNKS = 2
STREAMS = 2
HALVES = 2
PIECES = 1
EXCHANGE = 3


def gelu_and_slope(value):
    below = 0.5 * (1.0 + lax.erf(value / math.sqrt(2.0)))
    density = jnp.exp(-0.5 * value * value) / math.sqrt(2.0 * math.pi)
    return value * below, below + value * density


def tile(extent, limit):
    best = 128
    for size in range(128, min(extent, limit) + 1, 128):
        if extent % size == 0:
            best = size
    return best


chain = []


def chained_call(body, name, grid, flops, moved, in_specs, out_specs, out_shape, vmem=24, prefetch=0, **spec):
    several = isinstance(out_specs, list)
    outs = out_specs if several else [out_specs]
    shapes = out_shape if several else [out_shape]
    token = jax.ShapeDtypeStruct((8, 128), F32)

    def with_token(*refs):
        ends = prefetch + len(in_specs), prefetch + len(in_specs) + 1 + len(outs)
        refs[ends[1]][...] = jnp.zeros((8, 128), F32)
        body(*refs[: ends[0]], *refs[ends[0] + 1 : ends[1]])

    def run(*args):
        *values, after = pl.pallas_call(
            with_token,
            grid_spec=pltpu.PrefetchScalarGridSpec(
                num_scalar_prefetch=prefetch,
                grid=grid,
                in_specs=in_specs + [pl.BlockSpec(memory_space=pl.ANY)],
                out_specs=outs + [pl.BlockSpec((8, 128), lambda *_: (0, 0))],
            ),
            out_shape=shapes + [token],
            compiler_params=pltpu.CompilerParams(vmem_limit_bytes=vmem * 2**20),
            cost_estimate=pl.CostEstimate(flops=flops, bytes_accessed=moved, transcendentals=0),
            name=name,
            **spec,
        )(*args, chain[-1])
        chain.append(after)
        return values if several else values[0]

    return run


def forward_matmul(x, weight, chunk, f):
    rows, width = x.shape
    bn = tile(f, 512)
    steps = f // bn
    part = rows // HALVES

    def body(x_ref, w_ref, *outs):
        total = jnp.dot(x_ref[...], w_ref[...], preferred_element_type=F32).astype(BF16)
        for half, out in enumerate(outs):
            out[...] = total[half * part : (half + 1) * part]

    return chained_call(
        body,
        "forward",
        (steps,),
        2 * rows * width * f,
        2 * (rows * width + width * f + rows * f),
        vmem=47,
        in_specs=[
            pl.BlockSpec((rows, width), lambda j: (0, 0)),
            pl.BlockSpec((width, bn), lambda j: (0, chunk * steps + j)),
        ],
        out_specs=[pl.BlockSpec((part, bn), lambda j: (0, j))] * HALVES,
        out_shape=[jax.ShapeDtypeStruct((part, f), BF16)] * HALVES,
    )(x, weight)


def input_grad_matmul(g, half, weight, chunk, total, buffer, last, first, pieces):
    rows, f = g.shape[0] // HALVES, g.shape[1]
    width = weight.shape[0]
    span = width // PIECES * pieces
    bn = tile(width // PIECES, 256)
    steps = span // bn
    start = first * (width // PIECES // bn)
    added = [] if total is None else [total]
    kept = [] if buffer is None else [buffer]

    def body(g_ref, w_ref, *rest):
        part = lax.dot_general(
            g_ref[...], w_ref[...], (((1,), (1,)), ((), ())), preferred_element_type=F32
        )
        if added:
            part += rest[0][...]
        rest[-1][...] = part.astype(rest[-1].dtype)

    out = pl.BlockSpec((rows, bn), lambda j: (0, start + j))
    return chained_call(
        body,
        "input_grad",
        (steps,),
        2 * rows * span * f,
        2 * (rows * f + span * f + 4 * rows * span),
        vmem=47,
        in_specs=[
            pl.BlockSpec((rows, f), lambda j: (half, 0)),
            pl.BlockSpec((bn, f), lambda j: (start + j, chunk)),
        ]
        + [out] * len(added)
        + [pl.BlockSpec(memory_space=pl.ANY)] * len(kept),
        out_specs=out,
        out_shape=jax.ShapeDtypeStruct((rows, width), BF16 if last else F32),
        input_output_aliases={2 + len(added): 0} if kept else {},
    )(g, weight, *added, *kept)


def weight_grad_matmul(x_t, g, buffer, chunk, units):
    width, rows = x_t.shape
    f = g.shape[1]
    bn = tile(f, 512)
    steps = f // bn
    kept = [] if buffer is None else [buffer]

    def body(x_ref, g_ref, *rest):
        part = jnp.dot(x_ref[...], g_ref[...], preferred_element_type=F32)
        rest[-1][...] = part.astype(BF16)

    return chained_call(
        body,
        "weight_grad",
        (steps,),
        2 * rows * width * f,
        2 * (rows * width + rows * f + width * f),
        vmem=47,
        in_specs=[
            pl.BlockSpec((width, rows), lambda j: (0, 0)),
            pl.BlockSpec((rows, bn), lambda j: (0, j)),
        ]
        + [pl.BlockSpec(memory_space=pl.ANY)] * len(kept),
        out_specs=pl.BlockSpec((width, bn), lambda j: (0, chunk * steps + j)),
        out_shape=jax.ShapeDtypeStruct((width, units), BF16),
        input_output_aliases={2: 0} if kept else {},
    )(x_t, g, *kept)


def message_kernel(where, part, theirs, came, keep):
    _, cores, few, f = part.shape
    bn = tile(f, 768)

    def body(where_ref, part_ref, theirs_ref, *rest):
        out = rest[-1]
        mine = part_ref[0].astype(F32) + theirs_ref[0].astype(F32)
        if came is not None:
            here = rest[0][...].astype(F32)
            summing = where_ref[1] > 0
            mine = jnp.where(summing, mine, here if keep else 0.0)
            if not keep:
                mine += here
        out[...] = mine.astype(BF16)

    block = pl.BlockSpec((1, cores, few, bn), lambda j, where: (where[0], 0, 0, j))
    flat = pl.BlockSpec((cores, few, bn), lambda j, where: (0, 0, j))
    given = [] if came is None else [came]
    return chained_call(
        body,
        "message",
        (f // bn,),
        0,
        0,
        prefetch=1,
        in_specs=[block, block] + [flat] * len(given),
        out_specs=flat,
        out_shape=jax.ShapeDtypeStruct((cores, few, f), BF16),
    )(where, part, theirs, *given)


def gelu_kernel(core, part, theirs, came, came_there, cotangent, cotangent_there, half, chunk, kept):
    _, cores, few, f = part.shape
    bn = tile(f, 512)
    steps = f // bn
    kept = [] if kept is None else [kept]

    def body(core_ref, part_ref, theirs_ref, came_ref, there_ref, mine_ref, other_ref, *rest):
        slope, activated = rest[-2:]
        first = core_ref[0] == 0
        values = []
        for c in range(cores):
            pre = part_ref[0, c].astype(F32) + theirs_ref[0, c].astype(F32)
            pre = pre + came_ref[c].astype(F32) + there_ref[c].astype(F32)
            value, grad = gelu_and_slope(pre)
            values.append(value)
            mine, other = mine_ref[...].astype(F32), other_ref[...].astype(F32)
            cot = jnp.where(first == (c == 0), mine, other)
            slope[c] = (cot * grad).astype(BF16)
        activated[...] = jnp.where(first, values[0], values[1]).astype(BF16)

    block = pl.BlockSpec((1, cores, few, bn), lambda j, core: (0, 0, 0, j))
    flat = pl.BlockSpec((cores, few, bn), lambda j, core: (0, 0, j))
    rows = pl.BlockSpec((few, bn), lambda j, core: (half, chunk * steps + j))
    return chained_call(
        body,
        "gelu",
        (steps,),
        0,
        0,
        prefetch=1,
        in_specs=[block, block, flat, flat, rows, rows]
        + [pl.BlockSpec(memory_space=pl.ANY)] * len(kept),
        out_specs=[flat, rows],
        out_shape=[
            jax.ShapeDtypeStruct((cores, few, f), BF16),
            jax.ShapeDtypeStruct(cotangent.shape, BF16),
        ],
        input_output_aliases={7: 1} if kept else {},
    )(core, part, theirs, came, came_there, cotangent, cotangent_there, *kept)


def collect_kernel(place, slope, mine, theirs, depth, half, buffer):
    cores, few, f = slope.shape
    bn = tile(f, 1024)
    kept = [] if buffer is None else [buffer]

    def body(place_ref, *refs):
        slope_ref, out = refs[0], refs[-1]
        mine_refs, their_refs = refs[1:depth], refs[depth : 2 * depth - 1]
        z, core = place_ref[0], place_ref[1]
        out[0, 0] = slope_ref[...]
        for j in range(1, depth):
            above = z + j < depth
            here = above == (core == 1)
            for down in (True, False):
                step = j if down else depth - j
                side = above if down else jnp.logical_not(above)

                @pl.when(side & here)
                def _():
                    out[0, j] = mine_refs[step - 1][...]

                @pl.when(side & jnp.logical_not(here))
                def _():
                    out[0, j] = their_refs[step - 1][...]

    flat = pl.BlockSpec((cores, few, bn), lambda j, place: (0, 0, j))
    return chained_call(
        body,
        "collect",
        (f // bn,),
        0,
        0,
        prefetch=1,
        in_specs=[flat] * (2 * depth - 1) + [pl.BlockSpec(memory_space=pl.ANY)] * len(kept),
        out_specs=pl.BlockSpec(
            (1, depth, cores, few, bn), lambda j, place: (half, 0, 0, 0, j)
        ),
        out_shape=jax.ShapeDtypeStruct((HALVES, depth, cores, few, f), BF16),
        input_output_aliases={2 * depth: 0} if kept else {},
    )(place, slope, *mine, *theirs, *kept)


def on_device(tokens, weight, cotangent):
    n_row, n_col = lax.axis_size("row"), lax.axis_size("col")
    depth = n_row // CORES
    row, col = lax.axis_index("row"), lax.axis_index("col")
    z, core = row // CORES, row % CORES
    place = jnp.where(core == 0, z, depth - 1 - z)
    width, units = weight.shape
    share = cotangent.shape[0]
    few = share // HALVES
    f = units // CHUNKS
    square = n_col == 4 and depth == 4

    def swap(value):
        return lax.ppermute(value, "row", [(r, r ^ 1) for r in range(n_row)])

    def onward(value, places):
        up = [(p * CORES, (p + 1) * CORES) for p in places]
        down = [((depth - 1 - p) * CORES + 1, (depth - 2 - p) * CORES + 1) for p in places]
        return lax.ppermute(value, "row", up + down)

    def cross(value, offset):
        return lax.ppermute(value, "col", [(c, c ^ offset) for c in range(4)])

    chain[:] = [jnp.zeros((8, 128), F32)]
    env = {"tokens": tokens, "cotangent": cotangent}

    def fence(*names):
        names = list(dict.fromkeys(n for n in names if n in env))
        for name, value in zip(names, lax.optimization_barrier([env[n] for n in names])):
            env[name] = value

    def gather():
        if square:
            mine = tokens.reshape(CORES, share, width)
            by_x, by_y = cross(mine, 1), cross(mine, 2)
            far = jnp.stack([cross(by_x[0], 2), cross(by_y[1], 1)])
            held = jnp.stack([mine, by_x, by_y, far])
            order = [col ^ ((z + j) % depth) for j in range(depth)]
        else:
            held = lax.all_gather(tokens, "col", axis=0, tiled=True)
            held = held.reshape(depth, CORES, share, width)
            order = [(z + j) % depth for j in range(depth)]
        blocks = [lax.dynamic_index_in_dim(held, b, 0, keepdims=False) for b in order]
        parts = [
            b[:, half * few : (half + 1) * few] for half in range(HALVES) for b in blocks
        ]
        env["x"] = jnp.concatenate(parts).reshape(HALVES * n_row * few, width)

    def columns_of(chunk):
        return slice(chunk * f, (chunk + 1) * f)

    sequence = [(half, chunk) for half in range(HALVES) for chunk in range(CHUNKS)]
    items = [sequence[q::STREAMS] for q in range(STREAMS)]
    count = len(sequence) // STREAMS
    steps = [(i, t) for i in range(count) for t in range(depth)]
    steps += [(count, t) for t in range(depth - 2)]

    input_grad, done = {}, []
    pending = []

    def forward(q):
        for i, part in enumerate(forward_matmul(env["x"], weight, q, f)):
            env["part", q, i] = part.reshape(depth, CORES, few, f)

    def exchange(q, i):
        env["theirs", q, i] = swap(env["part", q, i])
        pending.append(("theirs", q, i))

    def transpose():
        env["x_t"] = env["x"].T
        done.append("x_t")

    def backward_input(q, i, first=0, pieces=PIECES, before=None, last=False):
        half, chunk = items[q][i]
        if first == 0:
            collect(q, i)
        key = ("total", q, i)
        env[key] = input_grad_matmul(
            env["g", chunk].reshape(-1, f),
            half,
            weight,
            chunk,
            env.get(before),
            env.get(key),
            last,
            first,
            pieces,
        )
        done.append(key)

    def backward_weight(chunk):
        env["weight_grad"] = weight_grad_matmul(
            env["x_t"], env["g", chunk].reshape(-1, f), env.get("weight_grad"), chunk, units
        )

    def scatter_input(half, direct, total):
        pair = total.astype(BF16).reshape(depth, CORES, few, width)
        if direct:
            blocks = []
            for offset in range(4):
                at = ((col ^ offset) + depth - z) % depth
                block = lax.dynamic_index_in_dim(pair, at, 0, keepdims=False)
                blocks.append(cross(block, offset) if offset else block)
            input_grad[half] = sum(b.astype(F32) for b in blocks).astype(BF16)
        else:
            pair = lax.dynamic_slice(
                jnp.concatenate([pair, pair]), ((depth - z) % depth, 0, 0, 0), pair.shape
            )
            got = lax.psum_scatter(
                pair.reshape(n_col, -1, few, width), "col", scatter_dimension=0, tiled=True
            )
            input_grad[half] = got.reshape(-1, few, width)

    core_there = core.astype(jnp.int32).reshape(1)
    place_there = jnp.stack([z, core]).astype(jnp.int32)

    def gelu(q, i):
        half, chunk = items[q][i]
        env["slope", q, i], env["activated"] = gelu_kernel(
            core_there,
            env["part", q, i],
            env["theirs", q, i],
            env["came", q],
            env["came_there", q],
            cotangent,
            env["cotangent_there"],
            half,
            chunk,
            env.get("activated"),
        )
        done.append(("slope", q, i))

    def collect(q, i):
        half, chunk = items[q][i]
        order = range(1, depth)
        env["g", chunk] = collect_kernel(
            place_there,
            env["slope", q, i],
            [env["got", q, i, j] for j in order],
            [env["got_there", q, i, j] for j in order],
            depth,
            half,
            env.get(("g", chunk)),
        )

    def message(q, step):
        i, t = steps[step]
        if t == depth - 1:
            env["msg", q] = env["slope", q, i]
        elif i == count:
            env["msg", q] = env["came", q]
        else:
            at = jnp.where(core == 0, depth - 1 - t, t + 1)
            env["msg", q] = message_kernel(
                jnp.stack([at, place <= t]).astype(jnp.int32),
                env["part", q, i],
                env["theirs", q, i],
                None if i == 0 and t == 0 else env["came", q],
                t == 0,
            )

    def start(q, step):
        i, t = steps[step]
        first = t + 1 if i == count else 0
        last = t + 1 if (i == 0 and t < depth - 2) else depth - 1
        env["came", q] = onward(env["msg", q], range(first, last))

    def receive(q, i, t):
        env["got", q, i, t] = env["came", q]
        env["got_there", q, i, t] = swap(env["came", q])
        pending.append(("got_there", q, i, t))

    env["cotangent_there"] = swap(cotangent)
    gather()
    fence("x", "cotangent_there")
    for q in range(STREAMS):
        forward(q)
        exchange(q, 0)
        fence(("part", q, 0), "x")
    fence(("theirs", 0, 0), ("part", STREAMS - 1, 0))
    for q in range(STREAMS):
        message(q, 0)
        start(q, 0)
    done.clear()
    pending.clear()
    for step in range(len(steps)):
        i, t = steps[step]
        for q in range(STREAMS):
            env["chain"] = chain[-1]
            fence(("came", q), "chain", *done, *pending)
            chain[-1] = env["chain"]
            done.clear()
            pending.clear()
            if t == depth - 2:
                env["came_there", q] = swap(env["came", q])
                gelu(q, i)
            elif t == depth - 1:
                receive(q, i, 1)
            elif i > 0:
                receive(q, i - 1, t + 2)
            if step + 1 == len(steps):
                before = ("total", q - 1, count - 1)
                backward_input(q, count - 1, before=before, last=q == STREAMS - 1)
                continue
            if i == 1 and t == 0 and q == 0:
                fence(("came", q), "x")
                transpose()
            if i == 1 and t == depth - 1:
                fence(("came", q), ("got_there", q, 0, depth - 1))
                backward_input(q, 0)
            fence(("came", q), *done)
            done.clear()
            message(q, step + 1)
            start(q, step + 1)
            if EXCHANGE < 3 and step == EXCHANGE:
                fence(("msg", q), ("part", q, 1))
                exchange(q, 1)
            if EXCHANGE == 3 and step == 2 and q == 1:
                for p in range(STREAMS):
                    fence(("msg", q), ("part", p, 1))
                    exchange(p, 1)
        if t == 0 and i == count:
            total = sum(env["total", p, i - 2] for p in range(STREAMS))
            scatter_input(0, False, total)
    last_total = ("total", STREAMS - 1, count - 1)
    scatter_input(HALVES - 1, square, env[last_total])
    for chunk in range(CHUNKS):
        fence(("g", chunk), last_total)
        backward_weight(chunk)

    input_grad = jnp.concatenate([input_grad[h] for h in range(HALVES)], axis=-2)
    return env["activated"], input_grad.reshape(tokens.shape), env["weight_grad"]


def solution(mesh):
    return jax.shard_map(
        on_device,
        mesh=mesh,
        in_specs=(P("col", "row"), P("row", "col"), P("row", "col")),
        out_specs=(P("row", "col"), P("col", "row"), P("row", "col")),
        check_vma=False,
    )
```

```python
import math

import jax
import jax.numpy as jnp
from jax import lax
from jax.experimental import pallas as pl
from jax.experimental.pallas import tpu as pltpu
from jax.sharding import PartitionSpec as P

BF16 = jnp.bfloat16
F32 = jnp.float32
CORES = 2
CHUNKS = 2
STREAMS = 2
HALVES = 2


def gelu_and_slope(value):
    below = 0.5 * (1.0 + lax.erf(value / math.sqrt(2.0)))
    density = jnp.exp(-0.5 * value * value) / math.sqrt(2.0 * math.pi)
    return value * below, below + value * density


def tile(extent, limit):
    best = 128
    for size in range(128, min(extent, limit) + 1, 128):
        if extent % size == 0:
            best = size
    return best


def matmul_call(body, name, grid, flops, moved, vmem=28, **spec):
    if grid is not None:
        spec["grid"] = grid
    return pl.pallas_call(
        body,
        compiler_params=pltpu.CompilerParams(vmem_limit_bytes=vmem * 2**20),
        cost_estimate=pl.CostEstimate(flops=flops, bytes_accessed=moved, transcendentals=0),
        name=name,
        **spec,
    )


def forward_matmul(x, weight, chunk, f):
    rows, width = x.shape
    bn = tile(f, 512)
    steps = f // bn

    def body(x_ref, w_ref, out):
        out[...] = jnp.dot(x_ref[...], w_ref[...], preferred_element_type=F32).astype(BF16)

    return matmul_call(
        body,
        "forward",
        (steps,),
        2 * rows * width * f,
        2 * (rows * width + width * f + rows * f),
        vmem=47,
        in_specs=[
            pl.BlockSpec((rows, width), lambda j: (0, 0)),
            pl.BlockSpec((width, bn), lambda j: (0, chunk * steps + j)),
        ],
        out_specs=pl.BlockSpec((rows, bn), lambda j: (0, j)),
        out_shape=jax.ShapeDtypeStruct((rows, f), BF16),
    )(x, weight)


def input_grad_matmul(g, weight, chunk, total, last):
    rows, f = g.shape
    width = weight.shape[0]
    bn = tile(width, 256)
    kept = [] if total is None else [total]

    def body(g_ref, w_ref, *rest):
        part = lax.dot_general(
            g_ref[...], w_ref[...], (((1,), (1,)), ((), ())), preferred_element_type=F32
        )
        if kept:
            part += rest[0][...]
        rest[-1][...] = part.astype(rest[-1].dtype)

    return matmul_call(
        body,
        "input_grad",
        (width // bn,),
        2 * rows * width * f,
        2 * (rows * f + width * f + 4 * rows * width),
        vmem=47,
        in_specs=[
            pl.BlockSpec((rows, f), lambda j: (0, 0)),
            pl.BlockSpec((bn, f), lambda j: (j, chunk)),
        ]
        + [pl.BlockSpec((rows, bn), lambda j: (0, j))] * len(kept),
        out_specs=pl.BlockSpec((rows, bn), lambda j: (0, j)),
        out_shape=jax.ShapeDtypeStruct((rows, width), BF16 if last else F32),
    )(g, weight, *kept)


def weight_grad_matmul(lefts, rights, buffer, chunk, units):
    width, rows = lefts[0].shape
    f = rights[0].shape[1]
    bn = tile(f, 512)
    steps = f // bn
    n = len(lefts)
    kept = [] if buffer is None else [buffer]

    def body(*refs):
        total = jnp.dot(refs[0][...], refs[n][...], preferred_element_type=F32)
        for i in range(1, n):
            total += jnp.dot(refs[i][...], refs[n + i][...], preferred_element_type=F32)
        refs[-1][...] = total.astype(BF16)

    return matmul_call(
        body,
        "weight_grad",
        (steps,),
        2 * n * rows * width * f,
        2 * (n * rows * width + n * rows * f + width * f),
        vmem=56,
        in_specs=[pl.BlockSpec((width, rows), lambda j: (0, 0))] * n
        + [pl.BlockSpec((rows, bn), lambda j: (0, j))] * n
        + [pl.BlockSpec(memory_space=pl.ANY)] * len(kept),
        out_specs=pl.BlockSpec((width, bn), lambda j: (0, chunk * steps + j)),
        out_shape=jax.ShapeDtypeStruct((width, units), BF16),
        input_output_aliases={2 * n: 0} if kept else {},
    )(*lefts, *rights, *kept)


def message_kernel(where, part, theirs, came, keep):
    _, cores, few, f = part.shape
    bn = tile(f, 1536)

    def body(where_ref, part_ref, theirs_ref, *rest):
        out = rest[-1]
        mine = part_ref[0].astype(F32) + theirs_ref[0].astype(F32)
        if came is not None:
            here = rest[0][...].astype(F32)
            summing = where_ref[1] > 0
            mine = jnp.where(summing, mine, here if keep else 0.0)
            if not keep:
                mine += here
        out[...] = mine.astype(BF16)

    block = pl.BlockSpec((1, cores, few, bn), lambda j, where: (where[0], 0, 0, j))
    flat = pl.BlockSpec((cores, few, bn), lambda j, where: (0, 0, j))
    given = [] if came is None else [came]
    return matmul_call(
        body,
        "message",
        None,
        0,
        0,
        grid_spec=pltpu.PrefetchScalarGridSpec(
            num_scalar_prefetch=1,
            grid=(f // bn,),
            in_specs=[block, block] + [flat] * len(given),
            out_specs=flat,
        ),
        out_shape=jax.ShapeDtypeStruct((cores, few, f), BF16),
    )(where, part, theirs, *given)


def gelu_kernel(core, part, theirs, came, came_there, cotangent, cotangent_there, half, chunk, kept):
    _, cores, few, f = part.shape
    bn = tile(f, 512)
    steps = f // bn
    kept = [] if kept is None else [kept]

    def body(core_ref, part_ref, theirs_ref, came_ref, there_ref, mine_ref, other_ref, *rest):
        slope, activated = rest[-2:]
        first = core_ref[0] == 0
        values = []
        for c in range(cores):
            pre = part_ref[0, c].astype(F32) + theirs_ref[0, c].astype(F32)
            pre = pre + came_ref[c].astype(F32) + there_ref[c].astype(F32)
            value, grad = gelu_and_slope(pre)
            values.append(value)
            mine, other = mine_ref[...].astype(F32), other_ref[...].astype(F32)
            cot = jnp.where(first == (c == 0), mine, other)
            slope[c] = (cot * grad).astype(BF16)
        activated[...] = jnp.where(first, values[0], values[1]).astype(BF16)

    block = pl.BlockSpec((1, cores, few, bn), lambda j, core: (0, 0, 0, j))
    flat = pl.BlockSpec((cores, few, bn), lambda j, core: (0, 0, j))
    rows = pl.BlockSpec((few, bn), lambda j, core: (half, chunk * steps + j))
    return matmul_call(
        body,
        "gelu",
        None,
        0,
        0,
        grid_spec=pltpu.PrefetchScalarGridSpec(
            num_scalar_prefetch=1,
            grid=(steps,),
            in_specs=[block, block, flat, flat, rows, rows]
            + [pl.BlockSpec(memory_space=pl.ANY)] * len(kept),
            out_specs=[flat, rows],
        ),
        out_shape=[
            jax.ShapeDtypeStruct((cores, few, f), BF16),
            jax.ShapeDtypeStruct(cotangent.shape, BF16),
        ],
        input_output_aliases={7: 1} if kept else {},
    )(core, part, theirs, came, came_there, cotangent, cotangent_there, *kept)


def collect_kernel(place, slope, mine, theirs, depth):
    cores, few, f = slope.shape
    bn = tile(f, 1024)

    def body(place_ref, *refs):
        slope_ref, out = refs[0], refs[-1]
        mine_refs, their_refs = refs[1:depth], refs[depth : 2 * depth - 1]
        z, core = place_ref[0], place_ref[1]
        out[0] = slope_ref[...]
        for j in range(1, depth):
            above = z + j < depth
            here = above == (core == 1)
            for down in (True, False):
                step = j if down else depth - j
                side = above if down else jnp.logical_not(above)

                @pl.when(side & here)
                def _():
                    out[j] = mine_refs[step - 1][...]

                @pl.when(side & jnp.logical_not(here))
                def _():
                    out[j] = their_refs[step - 1][...]

    flat = pl.BlockSpec((cores, few, bn), lambda j, place: (0, 0, j))
    return matmul_call(
        body,
        "collect",
        None,
        0,
        0,
        vmem=56,
        grid_spec=pltpu.PrefetchScalarGridSpec(
            num_scalar_prefetch=1,
            grid=(f // bn,),
            in_specs=[flat] * (2 * depth - 1),
            out_specs=pl.BlockSpec((depth, cores, few, bn), lambda j, place: (0, 0, 0, j)),
        ),
        out_shape=jax.ShapeDtypeStruct((depth, *slope.shape), BF16),
    )(place, slope, *mine, *theirs)


def on_device(tokens, weight, cotangent):
    n_row, n_col = lax.axis_size("row"), lax.axis_size("col")
    depth = n_row // CORES
    row, col = lax.axis_index("row"), lax.axis_index("col")
    z, core = row // CORES, row % CORES
    place = jnp.where(core == 0, z, depth - 1 - z)
    width, units = weight.shape
    share = cotangent.shape[0]
    few = share // HALVES
    f = units // CHUNKS
    square = n_col == 4 and depth == 4

    def swap(value):
        return lax.ppermute(value, "row", [(r, r ^ 1) for r in range(n_row)])

    def onward(value, places):
        up = [(p * CORES, (p + 1) * CORES) for p in places]
        down = [((depth - 1 - p) * CORES + 1, (depth - 2 - p) * CORES + 1) for p in places]
        return lax.ppermute(value, "row", up + down)

    def cross(value, offset):
        return lax.ppermute(value, "col", [(c, c ^ offset) for c in range(4)])

    env = {"tokens": tokens, "cotangent": cotangent}

    def fence(*names):
        names = list(dict.fromkeys(n for n in names if n in env))
        for name, value in zip(names, lax.optimization_barrier([env[n] for n in names])):
            env[name] = value

    def gather_near(half):
        mine = env["tokens"].reshape(-1, share, width)[:, half * few : (half + 1) * few]
        env["mine"] = mine
        if square:
            env["by_x"], env["by_y"] = cross(mine, 1), cross(mine, 2)
        else:
            env["all"] = lax.all_gather(mine, "col", axis=0, tiled=True)

    def gather_far():
        if square:
            env["far_x"], env["far_y"] = cross(env["by_x"][0], 2), cross(env["by_y"][1], 1)

    def gather_end(half):
        if square:
            far = jnp.stack([env["far_x"], env["far_y"]])
            held = jnp.stack([env["mine"], env["by_x"], env["by_y"], far])
            order = [col ^ ((z + j) % depth) for j in range(depth)]
        else:
            held = env["all"].reshape(depth, CORES, few, width)
            order = [(z + j) % depth for j in range(depth)]
        blocks = [lax.dynamic_index_in_dim(held, b, 0, keepdims=False) for b in order]
        env["x", half] = jnp.concatenate(blocks).reshape(n_row * few, width)

    def columns_of(chunk):
        return slice(chunk * f, (chunk + 1) * f)

    sequence = [(half, chunk) for half in range(HALVES) for chunk in range(CHUNKS)]
    items = [sequence[q::STREAMS] for q in range(STREAMS)]
    count = len(sequence) // STREAMS
    steps = [(i, t) for i in range(count) for t in range(depth)]
    steps += [(count, t) for t in range(depth - 2)]

    input_grad, seen, done, pending = {}, {}, [], []

    def forward(q, i):
        half, chunk = items[q][i]
        part = forward_matmul(env["x", half], weight, chunk, f)
        env["part", q, i] = part.reshape(depth, CORES, few, f)
        env["theirs", q, i] = swap(env["part", q, i])
        done.append(("part", q, i))

    def transpose(half):
        env["x_t", half] = env["x", half].T
        done.append(("x_t", half))

    def backward_input(q, i):
        half, chunk = items[q][i]
        collect(q, i)
        seen["total", half] = seen.get(("total", half), 0) + 1
        last = seen["total", half] == CHUNKS
        env["total", half] = input_grad_matmul(
            env["g", half, chunk], weight, chunk, env.get(("total", half)), last
        )
        done.append(("total", half))

    def backward_weight(chunk):
        halves = range(HALVES)
        env["weight_grad"] = weight_grad_matmul(
            [env["x_t", h] for h in halves],
            [env["g", h, chunk] for h in halves],
            env.get("weight_grad"),
            chunk,
            units,
        )

    def scatter_input(half):
        pair = env["total", half].reshape(depth, CORES, few, width)
        if square:
            blocks = []
            for offset in range(4):
                at = ((col ^ offset) + depth - z) % depth
                block = lax.dynamic_index_in_dim(pair, at, 0, keepdims=False)
                blocks.append(cross(block, offset) if offset else block)
            input_grad[half] = sum(b.astype(F32) for b in blocks).astype(BF16)
        else:
            pair = lax.dynamic_slice(
                jnp.concatenate([pair, pair]), ((depth - z) % depth, 0, 0, 0), pair.shape
            )
            total = lax.psum_scatter(
                pair.reshape(n_col, -1, few, width), "col", scatter_dimension=0, tiled=True
            )
            input_grad[half] = total[0]

    core_there = core.astype(jnp.int32).reshape(1)
    place_there = jnp.stack([z, core]).astype(jnp.int32)

    def gelu(q, i):
        half, chunk = items[q][i]
        env["slope", q], env["activated"] = gelu_kernel(
            core_there,
            env["part", q, i],
            env["theirs", q, i],
            env["came", q],
            env["came_there", q],
            cotangent,
            env["cotangent_there"],
            half,
            chunk,
            env.get("activated"),
        )

    def collect(q, i):
        half, chunk = items[q][i]
        order = range(1, depth)
        g = collect_kernel(
            place_there,
            env["slope", q],
            [env["got", q, j] for j in order],
            [env["got_there", q, j] for j in order],
            depth,
        )
        env["g", half, chunk] = g.reshape(n_row * few, f)

    def message(q, step):
        i, t = steps[step]
        if t == depth - 1:
            env["msg", q] = env["slope", q]
        elif i == count:
            env["msg", q] = env["came", q]
        else:
            at = jnp.where(core == 0, depth - 1 - t, t + 1)
            env["msg", q] = message_kernel(
                jnp.stack([at, place <= t]).astype(jnp.int32),
                env["part", q, i],
                env["theirs", q, i],
                None if i == 0 and t == 0 else env["came", q],
                t == 0,
            )

    def start(q, step):
        i, t = steps[step]
        first = t + 1 if i == count else 0
        last = t + 1 if (i == 0 and t < depth - 2) else depth - 1
        env["came", q] = onward(env["msg", q], range(first, last))

    def receive(q, t):
        env["got", q, t] = env["came", q]
        env["got_there", q, t] = swap(env["came", q])
        pending.append(("got_there", q, t))

    gather_near(0)
    gather_far()
    gather_end(0)
    for q in range(STREAMS):
        forward(q, 0)
    for q in range(STREAMS):
        message(q, 0)
        fence(("msg", q), ("x", 0), "tokens", "cotangent")
        start(q, 0)
    done.clear()
    pending.clear()
    for step in range(len(steps)):
        i, t = steps[step]
        for q in range(STREAMS):
            fence(("came", q), *done, *pending, *(["tokens", "cotangent"] if step == 0 and q == 0 else []))
            done.clear()
            pending.clear()
            if t == depth - 2:
                env["came_there", q] = swap(env["came", q])
                gelu(q, i)
            elif t == depth - 1:
                receive(q, 1)
            elif i > 0:
                receive(q, t + 2)
            work = []
            if step + 1 < len(steps):
                message(q, step + 1)
                i_next, t_next = steps[step + 1]
                if t_next == depth - 2 and i_next + 1 < count:
                    work.append((forward, (q, i_next + 1), ("x", items[q][i_next + 1][0])))
                if t_next == 1 and i_next == 1 and q < HALVES:
                    work.append((transpose, (q,), ("x", q)))
                if t_next == depth - 2 and i_next > 0:
                    work.append((backward_input, (q, i_next - 1), ("got", q, depth - 1)))
                fence(("msg", q), *[name for _, _, name in work])
                start(q, step + 1)
            else:
                work.append((backward_input, (q, count - 1), None))
            if step == 1 and q == 0:
                fence("far_x", "far_y", "all", ("msg", q))
                gather_end(1)
            for piece, args, _ in work:
                piece(*args)
            if step == 0 and q == 0:
                env["cotangent_there"] = swap(env["cotangent"])
                gather_near(1)
            if step == 0 and q == STREAMS - 1:
                fence("by_x", "by_y", "all", ("msg", q))
                gather_far()
        if t == depth - 1 and i == count - 1:
            for half in range(HALVES - 1):
                scatter_input(half)
    scatter_input(HALVES - 1)
    for chunk in range(CHUNKS):
        fence(("g", HALVES - 1, chunk), ("total", HALVES - 1))
        backward_weight(chunk)

    input_grad = jnp.concatenate([input_grad[h] for h in range(HALVES)], axis=-2)
    return env["activated"], input_grad.reshape(tokens.shape), env["weight_grad"]


def solution(mesh):
    return jax.shard_map(
        on_device,
        mesh=mesh,
        in_specs=(P("col", "row"), P("row", "col"), P("row", "col")),
        out_specs=(P("row", "col"), P("col", "row"), P("row", "col")),
        check_vma=False,
    )
```

```python
import math

import jax
import jax.numpy as jnp
from jax import lax
from jax.experimental import pallas as pl
from jax.experimental.pallas import tpu as pltpu
from jax.sharding import PartitionSpec as P

BF16 = jnp.bfloat16
F32 = jnp.float32
CORES = 2
CHUNKS = 2
STREAMS = 2
HALVES = 2


def gelu_and_slope(value):
    below = 0.5 * (1.0 + lax.erf(value / math.sqrt(2.0)))
    density = jnp.exp(-0.5 * value * value) / math.sqrt(2.0 * math.pi)
    return value * below, below + value * density


def tile(extent, limit):
    best = 128
    for size in range(128, min(extent, limit) + 1, 128):
        if extent % size == 0:
            best = size
    return best


def matmul_call(body, name, grid, flops, moved, vmem=60, **spec):
    if grid is not None:
        spec["grid"] = grid
    return pl.pallas_call(
        body,
        compiler_params=pltpu.CompilerParams(vmem_limit_bytes=vmem * 2**20),
        cost_estimate=pl.CostEstimate(flops=flops, bytes_accessed=moved, transcendentals=0),
        name=name,
        **spec,
    )


def forward_matmul(x, weight, chunk, f):
    rows, width = x.shape
    bn = tile(f, 512)
    steps = f // bn

    def body(x_ref, w_ref, out):
        out[...] = jnp.dot(x_ref[...], w_ref[...], preferred_element_type=F32).astype(BF16)

    return matmul_call(
        body,
        "forward",
        (steps,),
        2 * rows * width * f,
        2 * (rows * width + width * f + rows * f),
        vmem=14,
        in_specs=[
            pl.BlockSpec((rows, width), lambda j: (0, 0)),
            pl.BlockSpec((width, bn), lambda j: (0, chunk * steps + j)),
        ],
        out_specs=pl.BlockSpec((rows, bn), lambda j: (0, j)),
        out_shape=jax.ShapeDtypeStruct((rows, f), BF16),
    )(x, weight)


def input_grad_matmul(g, weight, chunk, total, last):
    rows, f = g.shape
    width = weight.shape[0]
    bn = tile(width, 256)
    kept = [] if total is None else [total]

    def body(g_ref, w_ref, *rest):
        part = lax.dot_general(
            g_ref[...], w_ref[...], (((1,), (1,)), ((), ())), preferred_element_type=F32
        )
        if kept:
            part += rest[0][...]
        rest[-1][...] = part.astype(rest[-1].dtype)

    return matmul_call(
        body,
        "input_grad",
        (width // bn,),
        2 * rows * width * f,
        2 * (rows * f + width * f + 4 * rows * width),
        vmem=16,
        in_specs=[
            pl.BlockSpec((rows, f), lambda j: (0, 0)),
            pl.BlockSpec((bn, f), lambda j: (j, chunk)),
        ]
        + [pl.BlockSpec((rows, bn), lambda j: (0, j))] * len(kept),
        out_specs=pl.BlockSpec((rows, bn), lambda j: (0, j)),
        out_shape=jax.ShapeDtypeStruct((rows, width), BF16 if last else F32),
    )(g, weight, *kept)


def weight_grad_matmul(lefts, rights, buffer, chunk, units):
    width, rows = lefts[0].shape
    f = rights[0].shape[1]
    bn = tile(f, 512)
    steps = f // bn
    n = len(lefts)
    kept = [] if buffer is None else [buffer]

    def body(*refs):
        total = jnp.dot(refs[0][...], refs[n][...], preferred_element_type=F32)
        for i in range(1, n):
            total += jnp.dot(refs[i][...], refs[n + i][...], preferred_element_type=F32)
        refs[-1][...] = total.astype(BF16)

    return matmul_call(
        body,
        "weight_grad",
        (steps,),
        2 * n * rows * width * f,
        2 * (n * rows * width + n * rows * f + width * f),
        vmem=24,
        in_specs=[pl.BlockSpec((width, rows), lambda j: (0, 0))] * n
        + [pl.BlockSpec((rows, bn), lambda j: (0, j))] * n
        + [pl.BlockSpec(memory_space=pl.ANY)] * len(kept),
        out_specs=pl.BlockSpec((width, bn), lambda j: (0, chunk * steps + j)),
        out_shape=jax.ShapeDtypeStruct((width, units), BF16),
        input_output_aliases={2 * n: 0} if kept else {},
    )(*lefts, *rights, *kept)


def message_kernel(where, part, theirs, came, keep):
    _, cores, few, f = part.shape
    bn = tile(f, 1536)

    def body(where_ref, part_ref, theirs_ref, *rest):
        out = rest[-1]
        mine = part_ref[0].astype(F32) + theirs_ref[0].astype(F32)
        if came is not None:
            here = rest[0][...].astype(F32)
            summing = where_ref[1] > 0
            mine = jnp.where(summing, mine, here if keep else 0.0)
            if not keep:
                mine += here
        out[...] = mine.astype(BF16)

    block = pl.BlockSpec((1, cores, few, bn), lambda j, where: (where[0], 0, 0, j))
    flat = pl.BlockSpec((cores, few, bn), lambda j, where: (0, 0, j))
    given = [] if came is None else [came]
    return matmul_call(
        body,
        "message",
        None,
        0,
        0,
        vmem=8,
        grid_spec=pltpu.PrefetchScalarGridSpec(
            num_scalar_prefetch=1,
            grid=(f // bn,),
            in_specs=[block, block] + [flat] * len(given),
            out_specs=flat,
        ),
        out_shape=jax.ShapeDtypeStruct((cores, few, f), BF16),
    )(where, part, theirs, *given)


def gelu_kernel(core, part, theirs, came, came_there, cotangent, cotangent_there, half, chunk, kept):
    _, cores, few, f = part.shape
    bn = tile(f, 512)
    steps = f // bn
    kept = [] if kept is None else [kept]

    def body(core_ref, part_ref, theirs_ref, came_ref, there_ref, mine_ref, other_ref, *rest):
        slope, activated = rest[-2:]
        first = core_ref[0] == 0
        values = []
        for c in range(cores):
            pre = part_ref[0, c].astype(F32) + theirs_ref[0, c].astype(F32)
            pre = pre + came_ref[c].astype(F32) + there_ref[c].astype(F32)
            value, grad = gelu_and_slope(pre)
            values.append(value)
            mine, other = mine_ref[...].astype(F32), other_ref[...].astype(F32)
            cot = jnp.where(first == (c == 0), mine, other)
            slope[c] = (cot * grad).astype(BF16)
        activated[...] = jnp.where(first, values[0], values[1]).astype(BF16)

    block = pl.BlockSpec((1, cores, few, bn), lambda j, core: (0, 0, 0, j))
    flat = pl.BlockSpec((cores, few, bn), lambda j, core: (0, 0, j))
    rows = pl.BlockSpec((few, bn), lambda j, core: (half, chunk * steps + j))
    return matmul_call(
        body,
        "gelu",
        None,
        0,
        0,
        vmem=8,
        grid_spec=pltpu.PrefetchScalarGridSpec(
            num_scalar_prefetch=1,
            grid=(steps,),
            in_specs=[block, block, flat, flat, rows, rows]
            + [pl.BlockSpec(memory_space=pl.ANY)] * len(kept),
            out_specs=[flat, rows],
        ),
        out_shape=[
            jax.ShapeDtypeStruct((cores, few, f), BF16),
            jax.ShapeDtypeStruct(cotangent.shape, BF16),
        ],
        input_output_aliases={7: 1} if kept else {},
    )(core, part, theirs, came, came_there, cotangent, cotangent_there, *kept)


def collect_kernel(place, slope, mine, theirs, depth):
    def body(place_ref, *refs):
        slope_ref, out, sems = refs[0], refs[-2], refs[-1]
        mine_refs, their_refs = refs[1:depth], refs[depth : 2 * depth - 1]
        z, core = place_ref[0], place_ref[1]
        pltpu.make_async_copy(slope_ref, out.at[0], sems.at[0]).start()
        for j in range(1, depth):
            above = z + j < depth
            here = above == (core == 1)
            for down in (True, False):
                step = j if down else depth - j
                side = above if down else jnp.logical_not(above)

                @pl.when(side & here)
                def _():
                    pltpu.make_async_copy(mine_refs[step - 1], out.at[j], sems.at[j]).start()

                @pl.when(side & jnp.logical_not(here))
                def _():
                    pltpu.make_async_copy(their_refs[step - 1], out.at[j], sems.at[j]).start()

        for j in range(depth):
            pltpu.make_async_copy(slope_ref, out.at[j], sems.at[j]).wait()

    shape = (depth, *slope.shape)
    return matmul_call(
        body,
        "collect",
        None,
        0,
        0,
        vmem=10,
        grid_spec=pltpu.PrefetchScalarGridSpec(
            num_scalar_prefetch=1,
            grid=(1,),
            in_specs=[pl.BlockSpec(memory_space=pl.ANY)] * (2 * depth - 1),
            out_specs=pl.BlockSpec(shape, lambda j, place: (0, 0, 0, 0)),
            scratch_shapes=[pltpu.SemaphoreType.DMA((depth,))],
        ),
        out_shape=jax.ShapeDtypeStruct(shape, BF16),
    )(place, slope, *mine, *theirs)


def on_device(tokens, weight, cotangent):
    n_row, n_col = lax.axis_size("row"), lax.axis_size("col")
    depth = n_row // CORES
    row, col = lax.axis_index("row"), lax.axis_index("col")
    z, core = row // CORES, row % CORES
    place = jnp.where(core == 0, z, depth - 1 - z)
    width, units = weight.shape
    share = cotangent.shape[0]
    few = share // HALVES
    f = units // CHUNKS
    square = n_col == 4 and depth == 4

    def swap(value):
        return lax.ppermute(value, "row", [(r, r ^ 1) for r in range(n_row)])

    def onward(value, places):
        up = [(p * CORES, (p + 1) * CORES) for p in places]
        down = [((depth - 1 - p) * CORES + 1, (depth - 2 - p) * CORES + 1) for p in places]
        return lax.ppermute(value, "row", up + down)

    def cross(value, offset):
        return lax.ppermute(value, "col", [(c, c ^ offset) for c in range(4)])

    env = {"tokens": tokens, "cotangent": cotangent}

    def fence(*names):
        names = list(dict.fromkeys(n for n in names if n in env))
        for name, value in zip(names, lax.optimization_barrier([env[n] for n in names])):
            env[name] = value

    def gather_near(half):
        mine = env["tokens"].reshape(-1, share, width)[:, half * few : (half + 1) * few]
        env["mine"] = mine
        if square:
            env["by_x"], env["by_y"] = cross(mine, 1), cross(mine, 2)
        else:
            env["all"] = lax.all_gather(mine, "col", axis=0, tiled=True)

    def gather_far():
        if square:
            env["far_x"], env["far_y"] = cross(env["by_x"][0], 2), cross(env["by_y"][1], 1)

    def gather_end(half):
        if square:
            far = jnp.stack([env["far_x"], env["far_y"]])
            held = jnp.stack([env["mine"], env["by_x"], env["by_y"], far])
            order = [col ^ ((z + j) % depth) for j in range(depth)]
        else:
            held = env["all"].reshape(depth, CORES, few, width)
            order = [(z + j) % depth for j in range(depth)]
        blocks = [lax.dynamic_index_in_dim(held, b, 0, keepdims=False) for b in order]
        env["x", half] = jnp.concatenate(blocks).reshape(n_row * few, width)

    def columns_of(chunk):
        return slice(chunk * f, (chunk + 1) * f)

    sequence = [(half, chunk) for half in range(HALVES) for chunk in range(CHUNKS)]
    items = [sequence[q::STREAMS] for q in range(STREAMS)]
    count = len(sequence) // STREAMS
    steps = [(i, t) for i in range(count) for t in range(depth)]
    steps += [(count, t) for t in range(depth - 2)]

    input_grad, seen, done, pending = {}, {}, [], []

    def forward(q, i):
        half, chunk = items[q][i]
        part = forward_matmul(env["x", half], weight, chunk, f)
        env["part", q, i] = part.reshape(depth, CORES, few, f)
        env["theirs", q, i] = swap(env["part", q, i])
        done.append(("part", q, i))

    def transpose(half):
        env["x_t", half] = env["x", half].T
        done.append(("x_t", half))

    def backward_input(q, i):
        half, chunk = items[q][i]
        collect(q, i)
        seen["total", half] = seen.get(("total", half), 0) + 1
        last = seen["total", half] == CHUNKS
        env["total", half] = input_grad_matmul(
            env["g", half, chunk], weight, chunk, env.get(("total", half)), last
        )
        done.append(("total", half))

    def backward_weight(chunk):
        halves = range(HALVES)
        env["weight_grad"] = weight_grad_matmul(
            [env["x_t", h] for h in halves],
            [env["g", h, chunk] for h in halves],
            env.get("weight_grad"),
            chunk,
            units,
        )

    def scatter_input(half, direct):
        pair = env["total", half].reshape(depth, CORES, few, width)
        if direct:
            blocks = []
            for offset in range(4):
                at = ((col ^ offset) + depth - z) % depth
                block = lax.dynamic_index_in_dim(pair, at, 0, keepdims=False)
                blocks.append(cross(block, offset) if offset else block)
            input_grad[half] = sum(b.astype(F32) for b in blocks).astype(BF16)
        else:
            pair = lax.dynamic_slice(
                jnp.concatenate([pair, pair]), ((depth - z) % depth, 0, 0, 0), pair.shape
            )
            total = lax.psum_scatter(
                pair.reshape(n_col, -1, few, width), "col", scatter_dimension=0, tiled=True
            )
            input_grad[half] = total.reshape(-1, few, width)

    core_there = core.astype(jnp.int32).reshape(1)
    place_there = jnp.stack([z, core]).astype(jnp.int32)

    def gelu(q, i):
        half, chunk = items[q][i]
        env["slope", q], env["activated"] = gelu_kernel(
            core_there,
            env["part", q, i],
            env["theirs", q, i],
            env["came", q],
            env["came_there", q],
            cotangent,
            env["cotangent_there"],
            half,
            chunk,
            env.get("activated"),
        )

    def collect(q, i):
        half, chunk = items[q][i]
        order = range(1, depth)
        g = collect_kernel(
            place_there,
            env["slope", q],
            [env["got", q, j] for j in order],
            [env["got_there", q, j] for j in order],
            depth,
        )
        env["g", half, chunk] = g.reshape(n_row * few, f)

    def message(q, step):
        i, t = steps[step]
        if t == depth - 1:
            env["msg", q] = env["slope", q]
        elif i == count:
            env["msg", q] = env["came", q]
        else:
            at = jnp.where(core == 0, depth - 1 - t, t + 1)
            env["msg", q] = message_kernel(
                jnp.stack([at, place <= t]).astype(jnp.int32),
                env["part", q, i],
                env["theirs", q, i],
                None if i == 0 and t == 0 else env["came", q],
                t == 0,
            )

    def start(q, step):
        i, t = steps[step]
        first = t + 1 if i == count else 0
        last = t + 1 if (i == 0 and t < depth - 2) else depth - 1
        env["came", q] = onward(env["msg", q], range(first, last))

    def receive(q, t):
        env["got", q, t] = env["came", q]
        env["got_there", q, t] = swap(env["came", q])
        pending.append(("got_there", q, t))

    gather_near(0)
    gather_far()
    gather_end(0)
    for q in range(STREAMS):
        forward(q, 0)
    for q in range(STREAMS):
        message(q, 0)
        fence(("msg", q), ("x", 0), "tokens", "cotangent")
        start(q, 0)
    done.clear()
    pending.clear()
    for step in range(len(steps)):
        i, t = steps[step]
        for q in range(STREAMS):
            fence(("came", q), *done, *pending, *(["tokens", "cotangent"] if step == 0 and q == 0 else []))
            done.clear()
            pending.clear()
            if t == depth - 2:
                env["came_there", q] = swap(env["came", q])
                gelu(q, i)
            elif t == depth - 1:
                receive(q, 1)
            elif i > 0:
                receive(q, t + 2)
            work = []
            if step + 1 < len(steps):
                message(q, step + 1)
                i_next, t_next = steps[step + 1]
                if t_next == depth - 2 and i_next + 1 < count:
                    work.append((forward, (q, i_next + 1), ("x", items[q][i_next + 1][0])))
                if t_next == 1 and i_next == 1 and q < HALVES:
                    work.append((transpose, (q,), ("x", q)))
                if t_next == depth - 2 and i_next > 0:
                    work.append((backward_input, (q, i_next - 1), ("got", q, depth - 1)))
                fence(("msg", q), *[name for _, _, name in work])
                start(q, step + 1)
            else:
                work.append((backward_input, (q, count - 1), None))
            if step == 1 and q == 0:
                fence("far_x", "far_y", "all", ("msg", q))
                gather_end(1)
            for piece, args, _ in work:
                piece(*args)
            if step == 0 and q == 0:
                env["cotangent_there"] = swap(env["cotangent"])
                gather_near(1)
            if step == 0 and q == STREAMS - 1:
                fence("by_x", "by_y", "all", ("msg", q))
                gather_far()
        if t == depth - 1 and i == count - 1:
            for half in range(HALVES - 1):
                scatter_input(half, False)
    scatter_input(HALVES - 1, square)
    for chunk in range(CHUNKS):
        fence(("g", HALVES - 1, chunk), ("total", HALVES - 1))
        backward_weight(chunk)

    input_grad = jnp.concatenate([input_grad[h] for h in range(HALVES)], axis=-2)
    return env["activated"], input_grad.reshape(tokens.shape), env["weight_grad"]


def solution(mesh):
    return jax.shard_map(
        on_device,
        mesh=mesh,
        in_specs=(P("col", "row"), P("row", "col"), P("row", "col")),
        out_specs=(P("row", "col"), P("col", "row"), P("row", "col")),
        check_vma=False,
    )
```

```python
import math

import jax
import jax.numpy as jnp
from jax import lax
from jax.experimental import pallas as pl
from jax.experimental.pallas import tpu as pltpu
from jax.sharding import PartitionSpec as P

BF16 = jnp.bfloat16
F32 = jnp.float32
CORES = 2
CHUNKS = 2
STREAMS = 2
HALVES = 2


def gelu_and_slope(value):
    below = 0.5 * (1.0 + lax.erf(value / math.sqrt(2.0)))
    density = jnp.exp(-0.5 * value * value) / math.sqrt(2.0 * math.pi)
    return value * below, below + value * density


def tile(extent, limit):
    best = 128
    for size in range(128, min(extent, limit) + 1, 128):
        if extent % size == 0:
            best = size
    return best


def matmul_call(body, name, grid, flops, moved, vmem=60, **spec):
    if grid is not None:
        spec["grid"] = grid
    return pl.pallas_call(
        body,
        compiler_params=pltpu.CompilerParams(vmem_limit_bytes=vmem * 2**20),
        cost_estimate=pl.CostEstimate(flops=flops, bytes_accessed=moved, transcendentals=0),
        name=name,
        **spec,
    )


def forward_matmul(x, weight, chunk, f):
    rows, width = x.shape
    bn = tile(f, 512)
    steps = f // bn

    def body(x_ref, w_ref, out):
        out[...] = jnp.dot(x_ref[...], w_ref[...], preferred_element_type=F32).astype(BF16)

    return matmul_call(
        body,
        "forward",
        (steps,),
        2 * rows * width * f,
        2 * (rows * width + width * f + rows * f),
        vmem=47,
        in_specs=[
            pl.BlockSpec((rows, width), lambda j: (0, 0)),
            pl.BlockSpec((width, bn), lambda j: (0, chunk * steps + j)),
        ],
        out_specs=pl.BlockSpec((rows, bn), lambda j: (0, j)),
        out_shape=jax.ShapeDtypeStruct((rows, f), BF16),
    )(x, weight)


def input_grad_matmul(g, weight, chunk, total, last):
    rows, f = g.shape
    width = weight.shape[0]
    bn = tile(width, 256)
    kept = [] if total is None else [total]

    def body(g_ref, w_ref, *rest):
        part = lax.dot_general(
            g_ref[...], w_ref[...], (((1,), (1,)), ((), ())), preferred_element_type=F32
        )
        if kept:
            part += rest[0][...]
        rest[-1][...] = part.astype(rest[-1].dtype)

    return matmul_call(
        body,
        "input_grad",
        (width // bn,),
        2 * rows * width * f,
        2 * (rows * f + width * f + 4 * rows * width),
        vmem=47,
        in_specs=[
            pl.BlockSpec((rows, f), lambda j: (0, 0)),
            pl.BlockSpec((bn, f), lambda j: (j, chunk)),
        ]
        + [pl.BlockSpec((rows, bn), lambda j: (0, j))] * len(kept),
        out_specs=pl.BlockSpec((rows, bn), lambda j: (0, j)),
        out_shape=jax.ShapeDtypeStruct((rows, width), BF16 if last else F32),
    )(g, weight, *kept)


def weight_grad_matmul(lefts, rights, buffer, chunk, units):
    width, rows = lefts[0].shape
    f = rights[0].shape[1]
    bn = tile(f, 512)
    steps = f // bn
    n = len(lefts)
    kept = [] if buffer is None else [buffer]

    def body(*refs):
        total = jnp.dot(refs[0][...], refs[n][...], preferred_element_type=F32)
        for i in range(1, n):
            total += jnp.dot(refs[i][...], refs[n + i][...], preferred_element_type=F32)
        refs[-1][...] = total.astype(BF16)

    return matmul_call(
        body,
        "weight_grad",
        (steps,),
        2 * n * rows * width * f,
        2 * (n * rows * width + n * rows * f + width * f),
        vmem=24,
        in_specs=[pl.BlockSpec((width, rows), lambda j: (0, 0))] * n
        + [pl.BlockSpec((rows, bn), lambda j: (0, j))] * n
        + [pl.BlockSpec(memory_space=pl.ANY)] * len(kept),
        out_specs=pl.BlockSpec((width, bn), lambda j: (0, chunk * steps + j)),
        out_shape=jax.ShapeDtypeStruct((width, units), BF16),
        input_output_aliases={2 * n: 0} if kept else {},
    )(*lefts, *rights, *kept)


def message_kernel(where, part, theirs, came, keep):
    _, cores, few, f = part.shape
    bn = tile(f, 1536)

    def body(where_ref, part_ref, theirs_ref, *rest):
        out = rest[-1]
        mine = part_ref[0].astype(F32) + theirs_ref[0].astype(F32)
        if came is not None:
            here = rest[0][...].astype(F32)
            summing = where_ref[1] > 0
            mine = jnp.where(summing, mine, here if keep else 0.0)
            if not keep:
                mine += here
        out[...] = mine.astype(BF16)

    block = pl.BlockSpec((1, cores, few, bn), lambda j, where: (where[0], 0, 0, j))
    flat = pl.BlockSpec((cores, few, bn), lambda j, where: (0, 0, j))
    given = [] if came is None else [came]
    return matmul_call(
        body,
        "message",
        None,
        0,
        0,
        vmem=8,
        grid_spec=pltpu.PrefetchScalarGridSpec(
            num_scalar_prefetch=1,
            grid=(f // bn,),
            in_specs=[block, block] + [flat] * len(given),
            out_specs=flat,
        ),
        out_shape=jax.ShapeDtypeStruct((cores, few, f), BF16),
    )(where, part, theirs, *given)


def gelu_kernel(core, part, theirs, came, came_there, cotangent, cotangent_there, half, chunk, kept):
    _, cores, few, f = part.shape
    bn = tile(f, 512)
    steps = f // bn
    kept = [] if kept is None else [kept]

    def body(core_ref, part_ref, theirs_ref, came_ref, there_ref, mine_ref, other_ref, *rest):
        slope, activated = rest[-2:]
        first = core_ref[0] == 0
        values = []
        for c in range(cores):
            pre = part_ref[0, c].astype(F32) + theirs_ref[0, c].astype(F32)
            pre = pre + came_ref[c].astype(F32) + there_ref[c].astype(F32)
            value, grad = gelu_and_slope(pre)
            values.append(value)
            mine, other = mine_ref[...].astype(F32), other_ref[...].astype(F32)
            cot = jnp.where(first == (c == 0), mine, other)
            slope[c] = (cot * grad).astype(BF16)
        activated[...] = jnp.where(first, values[0], values[1]).astype(BF16)

    block = pl.BlockSpec((1, cores, few, bn), lambda j, core: (0, 0, 0, j))
    flat = pl.BlockSpec((cores, few, bn), lambda j, core: (0, 0, j))
    rows = pl.BlockSpec((few, bn), lambda j, core: (half, chunk * steps + j))
    return matmul_call(
        body,
        "gelu",
        None,
        0,
        0,
        vmem=8,
        grid_spec=pltpu.PrefetchScalarGridSpec(
            num_scalar_prefetch=1,
            grid=(steps,),
            in_specs=[block, block, flat, flat, rows, rows]
            + [pl.BlockSpec(memory_space=pl.ANY)] * len(kept),
            out_specs=[flat, rows],
        ),
        out_shape=[
            jax.ShapeDtypeStruct((cores, few, f), BF16),
            jax.ShapeDtypeStruct(cotangent.shape, BF16),
        ],
        input_output_aliases={7: 1} if kept else {},
    )(core, part, theirs, came, came_there, cotangent, cotangent_there, *kept)


def collect_kernel(place, slope, mine, theirs, depth):
    def body(place_ref, *refs):
        slope_ref, out, sems = refs[0], refs[-2], refs[-1]
        mine_refs, their_refs = refs[1:depth], refs[depth : 2 * depth - 1]
        z, core = place_ref[0], place_ref[1]
        pltpu.make_async_copy(slope_ref, out.at[0], sems.at[0]).start()
        for j in range(1, depth):
            above = z + j < depth
            here = above == (core == 1)
            for down in (True, False):
                step = j if down else depth - j
                side = above if down else jnp.logical_not(above)

                @pl.when(side & here)
                def _():
                    pltpu.make_async_copy(mine_refs[step - 1], out.at[j], sems.at[j]).start()

                @pl.when(side & jnp.logical_not(here))
                def _():
                    pltpu.make_async_copy(their_refs[step - 1], out.at[j], sems.at[j]).start()

        for j in range(depth):
            pltpu.make_async_copy(slope_ref, out.at[j], sems.at[j]).wait()

    shape = (depth, *slope.shape)
    return matmul_call(
        body,
        "collect",
        None,
        0,
        0,
        vmem=10,
        grid_spec=pltpu.PrefetchScalarGridSpec(
            num_scalar_prefetch=1,
            grid=(1,),
            in_specs=[pl.BlockSpec(memory_space=pl.ANY)] * (2 * depth - 1),
            out_specs=pl.BlockSpec(shape, lambda j, place: (0, 0, 0, 0)),
            scratch_shapes=[pltpu.SemaphoreType.DMA((depth,))],
        ),
        out_shape=jax.ShapeDtypeStruct(shape, BF16),
    )(place, slope, *mine, *theirs)


def on_device(tokens, weight, cotangent):
    n_row, n_col = lax.axis_size("row"), lax.axis_size("col")
    depth = n_row // CORES
    row, col = lax.axis_index("row"), lax.axis_index("col")
    z, core = row // CORES, row % CORES
    place = jnp.where(core == 0, z, depth - 1 - z)
    width, units = weight.shape
    share = cotangent.shape[0]
    few = share // HALVES
    f = units // CHUNKS
    square = n_col == 4 and depth == 4

    def swap(value):
        return lax.ppermute(value, "row", [(r, r ^ 1) for r in range(n_row)])

    def onward(value, places):
        up = [(p * CORES, (p + 1) * CORES) for p in places]
        down = [((depth - 1 - p) * CORES + 1, (depth - 2 - p) * CORES + 1) for p in places]
        return lax.ppermute(value, "row", up + down)

    def cross(value, offset):
        return lax.ppermute(value, "col", [(c, c ^ offset) for c in range(4)])

    env = {"tokens": tokens, "cotangent": cotangent}

    def fence(*names):
        names = list(dict.fromkeys(n for n in names if n in env))
        for name, value in zip(names, lax.optimization_barrier([env[n] for n in names])):
            env[name] = value

    def gather_near(half):
        mine = env["tokens"].reshape(-1, share, width)[:, half * few : (half + 1) * few]
        env["mine"] = mine
        if square:
            env["by_x"], env["by_y"] = cross(mine, 1), cross(mine, 2)
        else:
            env["all"] = lax.all_gather(mine, "col", axis=0, tiled=True)

    def gather_far():
        if square:
            env["far_x"], env["far_y"] = cross(env["by_x"][0], 2), cross(env["by_y"][1], 1)

    def gather_end(half):
        if square:
            far = jnp.stack([env["far_x"], env["far_y"]])
            held = jnp.stack([env["mine"], env["by_x"], env["by_y"], far])
            order = [col ^ ((z + j) % depth) for j in range(depth)]
        else:
            held = env["all"].reshape(depth, CORES, few, width)
            order = [(z + j) % depth for j in range(depth)]
        blocks = [lax.dynamic_index_in_dim(held, b, 0, keepdims=False) for b in order]
        env["x", half] = jnp.concatenate(blocks).reshape(n_row * few, width)

    def columns_of(chunk):
        return slice(chunk * f, (chunk + 1) * f)

    sequence = [(half, chunk) for half in range(HALVES) for chunk in range(CHUNKS)]
    items = [sequence[q::STREAMS] for q in range(STREAMS)]
    count = len(sequence) // STREAMS
    steps = [(i, t) for i in range(count) for t in range(depth)]
    steps += [(count, t) for t in range(depth - 2)]

    input_grad, seen, done, pending = {}, {}, [], []

    def forward(q, i):
        half, chunk = items[q][i]
        part = forward_matmul(env["x", half], weight, chunk, f)
        env["part", q, i] = part.reshape(depth, CORES, few, f)
        env["theirs", q, i] = swap(env["part", q, i])
        done.append(("part", q, i))

    def transpose(half):
        env["x_t", half] = env["x", half].T
        done.append(("x_t", half))

    def backward_input(q, i):
        half, chunk = items[q][i]
        collect(q, i)
        seen["total", half] = seen.get(("total", half), 0) + 1
        last = seen["total", half] == CHUNKS
        env["total", half] = input_grad_matmul(
            env["g", half, chunk], weight, chunk, env.get(("total", half)), last
        )
        done.append(("total", half))

    def backward_weight(chunk):
        halves = range(HALVES)
        env["weight_grad"] = weight_grad_matmul(
            [env["x_t", h] for h in halves],
            [env["g", h, chunk] for h in halves],
            env.get("weight_grad"),
            chunk,
            units,
        )

    def scatter_input(half, direct):
        pair = env["total", half].reshape(depth, CORES, few, width)
        if direct:
            blocks = []
            for offset in range(4):
                at = ((col ^ offset) + depth - z) % depth
                block = lax.dynamic_index_in_dim(pair, at, 0, keepdims=False)
                blocks.append(cross(block, offset) if offset else block)
            input_grad[half] = sum(b.astype(F32) for b in blocks).astype(BF16)
        else:
            pair = lax.dynamic_slice(
                jnp.concatenate([pair, pair]), ((depth - z) % depth, 0, 0, 0), pair.shape
            )
            total = lax.psum_scatter(
                pair.reshape(n_col, -1, few, width), "col", scatter_dimension=0, tiled=True
            )
            input_grad[half] = total.reshape(-1, few, width)

    core_there = core.astype(jnp.int32).reshape(1)
    place_there = jnp.stack([z, core]).astype(jnp.int32)

    def gelu(q, i):
        half, chunk = items[q][i]
        env["slope", q], env["activated"] = gelu_kernel(
            core_there,
            env["part", q, i],
            env["theirs", q, i],
            env["came", q],
            env["came_there", q],
            cotangent,
            env["cotangent_there"],
            half,
            chunk,
            env.get("activated"),
        )

    def collect(q, i):
        half, chunk = items[q][i]
        order = range(1, depth)
        g = collect_kernel(
            place_there,
            env["slope", q],
            [env["got", q, j] for j in order],
            [env["got_there", q, j] for j in order],
            depth,
        )
        env["g", half, chunk] = g.reshape(n_row * few, f)

    def message(q, step):
        i, t = steps[step]
        if t == depth - 1:
            env["msg", q] = env["slope", q]
        elif i == count:
            env["msg", q] = env["came", q]
        else:
            at = jnp.where(core == 0, depth - 1 - t, t + 1)
            env["msg", q] = message_kernel(
                jnp.stack([at, place <= t]).astype(jnp.int32),
                env["part", q, i],
                env["theirs", q, i],
                None if i == 0 and t == 0 else env["came", q],
                t == 0,
            )

    def start(q, step):
        i, t = steps[step]
        first = t + 1 if i == count else 0
        last = t + 1 if (i == 0 and t < depth - 2) else depth - 1
        env["came", q] = onward(env["msg", q], range(first, last))

    def receive(q, t):
        env["got", q, t] = env["came", q]
        env["got_there", q, t] = swap(env["came", q])
        pending.append(("got_there", q, t))

    gather_near(0)
    gather_far()
    gather_end(0)
    for q in range(STREAMS):
        forward(q, 0)
    for q in range(STREAMS):
        message(q, 0)
        fence(("msg", q), ("x", 0), "tokens", "cotangent")
        start(q, 0)
    done.clear()
    pending.clear()
    for step in range(len(steps)):
        i, t = steps[step]
        for q in range(STREAMS):
            fence(("came", q), *done, *pending, *(["tokens", "cotangent"] if step == 0 and q == 0 else []))
            done.clear()
            pending.clear()
            if t == depth - 2:
                env["came_there", q] = swap(env["came", q])
                gelu(q, i)
            elif t == depth - 1:
                receive(q, 1)
            elif i > 0:
                receive(q, t + 2)
            work = []
            if step + 1 < len(steps):
                message(q, step + 1)
                i_next, t_next = steps[step + 1]
                if t_next == depth - 2 and i_next + 1 < count:
                    work.append((forward, (q, i_next + 1), ("x", items[q][i_next + 1][0])))
                if t_next == 1 and i_next == 1 and q < HALVES:
                    work.append((transpose, (q,), ("x", q)))
                if t_next == depth - 2 and i_next > 0:
                    work.append((backward_input, (q, i_next - 1), ("got", q, depth - 1)))
                fence(("msg", q), *[name for _, _, name in work])
                start(q, step + 1)
            else:
                work.append((backward_input, (q, count - 1), None))
            if step == 1 and q == 0:
                fence("far_x", "far_y", "all", ("msg", q))
                gather_end(1)
            for piece, args, _ in work:
                piece(*args)
            if step == 0 and q == 0:
                env["cotangent_there"] = swap(env["cotangent"])
                gather_near(1)
            if step == 0 and q == STREAMS - 1:
                fence("by_x", "by_y", "all", ("msg", q))
                gather_far()
        if t == depth - 1 and i == count - 1:
            for half in range(HALVES - 1):
                scatter_input(half, False)
    scatter_input(HALVES - 1, square)
    for chunk in range(CHUNKS):
        fence(("g", HALVES - 1, chunk), ("total", HALVES - 1))
        backward_weight(chunk)

    input_grad = jnp.concatenate([input_grad[h] for h in range(HALVES)], axis=-2)
    return env["activated"], input_grad.reshape(tokens.shape), env["weight_grad"]


def solution(mesh):
    return jax.shard_map(
        on_device,
        mesh=mesh,
        in_specs=(P("col", "row"), P("row", "col"), P("row", "col")),
        out_specs=(P("row", "col"), P("col", "row"), P("row", "col")),
        check_vma=False,
    )
```

```python
import math

import jax
import jax.numpy as jnp
from jax import lax
from jax.experimental import pallas as pl
from jax.experimental.pallas import tpu as pltpu
from jax.sharding import PartitionSpec as P

BF16 = jnp.bfloat16
F32 = jnp.float32
CORES = 2
CHUNKS = 2
STREAMS = 2
HALVES = 2


def gelu_and_slope(value):
    below = 0.5 * (1.0 + lax.erf(value / math.sqrt(2.0)))
    density = jnp.exp(-0.5 * value * value) / math.sqrt(2.0 * math.pi)
    return value * below, below + value * density


def tile(extent, limit):
    best = 128
    for size in range(128, min(extent, limit) + 1, 128):
        if extent % size == 0:
            best = size
    return best


def matmul_call(body, name, grid, flops, moved, vmem=60, **spec):
    if grid is not None:
        spec["grid"] = grid
    return pl.pallas_call(
        body,
        compiler_params=pltpu.CompilerParams(vmem_limit_bytes=vmem * 2**20),
        cost_estimate=pl.CostEstimate(flops=flops, bytes_accessed=moved, transcendentals=0),
        name=name,
        **spec,
    )


def forward_matmul(x, weight, chunk, f):
    rows, width = x.shape
    bn = tile(f, 512)
    steps = f // bn

    def body(x_ref, w_ref, out):
        out[...] = jnp.dot(x_ref[...], w_ref[...], preferred_element_type=F32).astype(BF16)

    return matmul_call(
        body,
        "forward",
        (steps,),
        2 * rows * width * f,
        2 * (rows * width + width * f + rows * f),
        vmem=47,
        in_specs=[
            pl.BlockSpec((rows, width), lambda j: (0, 0)),
            pl.BlockSpec((width, bn), lambda j: (0, chunk * steps + j)),
        ],
        out_specs=pl.BlockSpec((rows, bn), lambda j: (0, j)),
        out_shape=jax.ShapeDtypeStruct((rows, f), BF16),
    )(x, weight)


def input_grad_matmul(g, weight, chunk, total, last):
    rows, f = g.shape
    width = weight.shape[0]
    bn = tile(width, 256)
    kept = [] if total is None else [total]

    def body(g_ref, w_ref, *rest):
        part = lax.dot_general(
            g_ref[...], w_ref[...], (((1,), (1,)), ((), ())), preferred_element_type=F32
        )
        if kept:
            part += rest[0][...]
        rest[-1][...] = part.astype(rest[-1].dtype)

    return matmul_call(
        body,
        "input_grad",
        (width // bn,),
        2 * rows * width * f,
        2 * (rows * f + width * f + 4 * rows * width),
        vmem=47,
        in_specs=[
            pl.BlockSpec((rows, f), lambda j: (0, 0)),
            pl.BlockSpec((bn, f), lambda j: (j, chunk)),
        ]
        + [pl.BlockSpec((rows, bn), lambda j: (0, j))] * len(kept),
        out_specs=pl.BlockSpec((rows, bn), lambda j: (0, j)),
        out_shape=jax.ShapeDtypeStruct((rows, width), BF16 if last else F32),
    )(g, weight, *kept)


def input_grad_whole(gs, weight):
    rows, f = gs[0].shape
    width, units = weight.shape
    bn = tile(width, 256)

    def body(*refs):
        g_refs, w_ref, out = refs[:-2], refs[-2], refs[-1]
        total = 0.0
        for chunk, g_ref in enumerate(g_refs):
            total += lax.dot_general(
                g_ref[...],
                w_ref[:, chunk * f : (chunk + 1) * f],
                (((1,), (1,)), ((), ())),
                preferred_element_type=F32,
            )
        out[...] = total.astype(BF16)

    return matmul_call(
        body,
        "input_grad_whole",
        (width // bn,),
        2 * rows * width * units,
        2 * (rows * units + width * units + rows * width),
        vmem=47,
        in_specs=[pl.BlockSpec((rows, f), lambda j: (0, 0))] * len(gs)
        + [pl.BlockSpec((bn, units), lambda j: (j, 0))],
        out_specs=pl.BlockSpec((rows, bn), lambda j: (0, j)),
        out_shape=jax.ShapeDtypeStruct((rows, width), BF16),
    )(*gs, weight)


def weight_grad_matmul(lefts, rights, buffer, chunk, units):
    width, rows = lefts[0].shape
    f = rights[0].shape[1]
    bn = tile(f, 512)
    steps = f // bn
    n = len(lefts)
    kept = [] if buffer is None else [buffer]

    def body(*refs):
        total = jnp.dot(refs[0][...], refs[n][...], preferred_element_type=F32)
        for i in range(1, n):
            total += jnp.dot(refs[i][...], refs[n + i][...], preferred_element_type=F32)
        refs[-1][...] = total.astype(BF16)

    return matmul_call(
        body,
        "weight_grad",
        (steps,),
        2 * n * rows * width * f,
        2 * (n * rows * width + n * rows * f + width * f),
        vmem=24,
        in_specs=[pl.BlockSpec((width, rows), lambda j: (0, 0))] * n
        + [pl.BlockSpec((rows, bn), lambda j: (0, j))] * n
        + [pl.BlockSpec(memory_space=pl.ANY)] * len(kept),
        out_specs=pl.BlockSpec((width, bn), lambda j: (0, chunk * steps + j)),
        out_shape=jax.ShapeDtypeStruct((width, units), BF16),
        input_output_aliases={2 * n: 0} if kept else {},
    )(*lefts, *rights, *kept)


def message_kernel(where, part, theirs, came, keep):
    _, cores, few, f = part.shape
    bn = tile(f, 1536)

    def body(where_ref, part_ref, theirs_ref, *rest):
        out = rest[-1]
        mine = part_ref[0].astype(F32) + theirs_ref[0].astype(F32)
        if came is not None:
            here = rest[0][...].astype(F32)
            summing = where_ref[1] > 0
            mine = jnp.where(summing, mine, here if keep else 0.0)
            if not keep:
                mine += here
        out[...] = mine.astype(BF16)

    block = pl.BlockSpec((1, cores, few, bn), lambda j, where: (where[0], 0, 0, j))
    flat = pl.BlockSpec((cores, few, bn), lambda j, where: (0, 0, j))
    given = [] if came is None else [came]
    return matmul_call(
        body,
        "message",
        None,
        0,
        0,
        vmem=8,
        grid_spec=pltpu.PrefetchScalarGridSpec(
            num_scalar_prefetch=1,
            grid=(f // bn,),
            in_specs=[block, block] + [flat] * len(given),
            out_specs=flat,
        ),
        out_shape=jax.ShapeDtypeStruct((cores, few, f), BF16),
    )(where, part, theirs, *given)


def gelu_kernel(core, part, theirs, came, came_there, cotangent, cotangent_there, half, chunk, kept):
    _, cores, few, f = part.shape
    bn = tile(f, 512)
    steps = f // bn
    kept = [] if kept is None else [kept]

    def body(core_ref, part_ref, theirs_ref, came_ref, there_ref, mine_ref, other_ref, *rest):
        slope, activated = rest[-2:]
        first = core_ref[0] == 0
        values = []
        for c in range(cores):
            pre = part_ref[0, c].astype(F32) + theirs_ref[0, c].astype(F32)
            pre = pre + came_ref[c].astype(F32) + there_ref[c].astype(F32)
            value, grad = gelu_and_slope(pre)
            values.append(value)
            mine, other = mine_ref[...].astype(F32), other_ref[...].astype(F32)
            cot = jnp.where(first == (c == 0), mine, other)
            slope[c] = (cot * grad).astype(BF16)
        activated[...] = jnp.where(first, values[0], values[1]).astype(BF16)

    block = pl.BlockSpec((1, cores, few, bn), lambda j, core: (0, 0, 0, j))
    flat = pl.BlockSpec((cores, few, bn), lambda j, core: (0, 0, j))
    rows = pl.BlockSpec((few, bn), lambda j, core: (half, chunk * steps + j))
    return matmul_call(
        body,
        "gelu",
        None,
        0,
        0,
        vmem=8,
        grid_spec=pltpu.PrefetchScalarGridSpec(
            num_scalar_prefetch=1,
            grid=(steps,),
            in_specs=[block, block, flat, flat, rows, rows]
            + [pl.BlockSpec(memory_space=pl.ANY)] * len(kept),
            out_specs=[flat, rows],
        ),
        out_shape=[
            jax.ShapeDtypeStruct((cores, few, f), BF16),
            jax.ShapeDtypeStruct(cotangent.shape, BF16),
        ],
        input_output_aliases={7: 1} if kept else {},
    )(core, part, theirs, came, came_there, cotangent, cotangent_there, *kept)


def collect_kernel(place, slope, mine, theirs, depth):
    def body(place_ref, *refs):
        slope_ref, out, sems = refs[0], refs[-2], refs[-1]
        mine_refs, their_refs = refs[1:depth], refs[depth : 2 * depth - 1]
        z, core = place_ref[0], place_ref[1]
        pltpu.make_async_copy(slope_ref, out.at[0], sems.at[0]).start()
        for j in range(1, depth):
            above = z + j < depth
            here = above == (core == 1)
            for down in (True, False):
                step = j if down else depth - j
                side = above if down else jnp.logical_not(above)

                @pl.when(side & here)
                def _():
                    pltpu.make_async_copy(mine_refs[step - 1], out.at[j], sems.at[j]).start()

                @pl.when(side & jnp.logical_not(here))
                def _():
                    pltpu.make_async_copy(their_refs[step - 1], out.at[j], sems.at[j]).start()

        for j in range(depth):
            pltpu.make_async_copy(slope_ref, out.at[j], sems.at[j]).wait()

    shape = (depth, *slope.shape)
    return matmul_call(
        body,
        "collect",
        None,
        0,
        0,
        vmem=47,
        grid_spec=pltpu.PrefetchScalarGridSpec(
            num_scalar_prefetch=1,
            grid=(1,),
            in_specs=[pl.BlockSpec(memory_space=pl.ANY)] * (2 * depth - 1),
            out_specs=pl.BlockSpec(shape, lambda j, place: (0, 0, 0, 0)),
            scratch_shapes=[pltpu.SemaphoreType.DMA((depth,))],
        ),
        out_shape=jax.ShapeDtypeStruct(shape, BF16),
    )(place, slope, *mine, *theirs)


def on_device(tokens, weight, cotangent):
    n_row, n_col = lax.axis_size("row"), lax.axis_size("col")
    depth = n_row // CORES
    row, col = lax.axis_index("row"), lax.axis_index("col")
    z, core = row // CORES, row % CORES
    place = jnp.where(core == 0, z, depth - 1 - z)
    width, units = weight.shape
    share = cotangent.shape[0]
    few = share // HALVES
    f = units // CHUNKS
    square = n_col == 4 and depth == 4

    def swap(value):
        return lax.ppermute(value, "row", [(r, r ^ 1) for r in range(n_row)])

    def onward(value, places):
        up = [(p * CORES, (p + 1) * CORES) for p in places]
        down = [((depth - 1 - p) * CORES + 1, (depth - 2 - p) * CORES + 1) for p in places]
        return lax.ppermute(value, "row", up + down)

    def cross(value, offset):
        return lax.ppermute(value, "col", [(c, c ^ offset) for c in range(4)])

    env = {"tokens": tokens, "cotangent": cotangent}

    def fence(*names):
        names = list(dict.fromkeys(n for n in names if n in env))
        for name, value in zip(names, lax.optimization_barrier([env[n] for n in names])):
            env[name] = value

    def gather_near(half):
        mine = env["tokens"].reshape(-1, share, width)[:, half * few : (half + 1) * few]
        env["mine"] = mine
        if square:
            env["by_x"], env["by_y"] = cross(mine, 1), cross(mine, 2)
        else:
            env["all"] = lax.all_gather(mine, "col", axis=0, tiled=True)

    def gather_far():
        if square:
            env["far_x"], env["far_y"] = cross(env["by_x"][0], 2), cross(env["by_y"][1], 1)

    def gather_end(half):
        if square:
            far = jnp.stack([env["far_x"], env["far_y"]])
            held = jnp.stack([env["mine"], env["by_x"], env["by_y"], far])
            order = [col ^ ((z + j) % depth) for j in range(depth)]
        else:
            held = env["all"].reshape(depth, CORES, few, width)
            order = [(z + j) % depth for j in range(depth)]
        blocks = [lax.dynamic_index_in_dim(held, b, 0, keepdims=False) for b in order]
        env["x", half] = jnp.concatenate(blocks).reshape(n_row * few, width)

    def columns_of(chunk):
        return slice(chunk * f, (chunk + 1) * f)

    sequence = [(half, chunk) for half in range(HALVES) for chunk in range(CHUNKS)]
    items = [sequence[q::STREAMS] for q in range(STREAMS)]
    count = len(sequence) // STREAMS
    steps = [(i, t) for i in range(count) for t in range(depth)]
    steps += [(count, t) for t in range(depth - 2)]

    input_grad, seen, done, pending = {}, {}, [], []

    def forward(q, i):
        half, chunk = items[q][i]
        part = forward_matmul(env["x", half], weight, chunk, f)
        env["part", q, i] = part.reshape(depth, CORES, few, f)
        env["theirs", q, i] = swap(env["part", q, i])
        done.append(("part", q, i))

    def transpose(half):
        env["x_t", half] = env["x", half].T
        done.append(("x_t", half))

    def backward_input(q, i):
        half, chunk = items[q][i]
        collect(q, i)
        seen["total", half] = seen.get(("total", half), 0) + 1
        last = seen["total", half] == CHUNKS
        env["total", half] = input_grad_matmul(
            env["g", half, chunk], weight, chunk, env.get(("total", half)), last
        )
        done.append(("total", half))

    def backward_half(q, i):
        collect(q, i)
        half = items[q][i][0]
        if q == STREAMS - 1:
            gs = [env["g", half, chunk] for chunk in range(CHUNKS)]
            env["total", half] = input_grad_whole(gs, weight)
            done.append(("total", half))
        else:
            done.append(("g", *items[q][i]))

    def backward_weight(chunk):
        halves = range(HALVES)
        env["weight_grad"] = weight_grad_matmul(
            [env["x_t", h] for h in halves],
            [env["g", h, chunk] for h in halves],
            env.get("weight_grad"),
            chunk,
            units,
        )

    def scatter_input(half, direct):
        pair = env["total", half].reshape(depth, CORES, few, width)
        if direct:
            blocks = []
            for offset in range(4):
                at = ((col ^ offset) + depth - z) % depth
                block = lax.dynamic_index_in_dim(pair, at, 0, keepdims=False)
                blocks.append(cross(block, offset) if offset else block)
            input_grad[half] = sum(b.astype(F32) for b in blocks).astype(BF16)
        else:
            pair = lax.dynamic_slice(
                jnp.concatenate([pair, pair]), ((depth - z) % depth, 0, 0, 0), pair.shape
            )
            total = lax.psum_scatter(
                pair.reshape(n_col, -1, few, width), "col", scatter_dimension=0, tiled=True
            )
            input_grad[half] = total.reshape(-1, few, width)

    core_there = core.astype(jnp.int32).reshape(1)
    place_there = jnp.stack([z, core]).astype(jnp.int32)

    def gelu(q, i):
        half, chunk = items[q][i]
        env["slope", q], env["activated"] = gelu_kernel(
            core_there,
            env["part", q, i],
            env["theirs", q, i],
            env["came", q],
            env["came_there", q],
            cotangent,
            env["cotangent_there"],
            half,
            chunk,
            env.get("activated"),
        )

    def collect(q, i):
        half, chunk = items[q][i]
        order = range(1, depth)
        g = collect_kernel(
            place_there,
            env["slope", q],
            [env["got", q, j] for j in order],
            [env["got_there", q, j] for j in order],
            depth,
        )
        env["g", half, chunk] = g.reshape(n_row * few, f)

    def message(q, step):
        i, t = steps[step]
        if t == depth - 1:
            env["msg", q] = env["slope", q]
        elif i == count:
            env["msg", q] = env["came", q]
        else:
            at = jnp.where(core == 0, depth - 1 - t, t + 1)
            env["msg", q] = message_kernel(
                jnp.stack([at, place <= t]).astype(jnp.int32),
                env["part", q, i],
                env["theirs", q, i],
                None if i == 0 and t == 0 else env["came", q],
                t == 0,
            )

    def start(q, step):
        i, t = steps[step]
        first = t + 1 if i == count else 0
        last = t + 1 if (i == 0 and t < depth - 2) else depth - 1
        env["came", q] = onward(env["msg", q], range(first, last))

    def receive(q, t):
        env["got", q, t] = env["came", q]
        env["got_there", q, t] = swap(env["came", q])
        pending.append(("got_there", q, t))

    gather_near(0)
    gather_far()
    gather_end(0)
    for q in range(STREAMS):
        forward(q, 0)
    for q in range(STREAMS):
        message(q, 0)
        fence(("msg", q), ("x", 0), "tokens", "cotangent")
        start(q, 0)
    done.clear()
    pending.clear()
    for step in range(len(steps)):
        i, t = steps[step]
        for q in range(STREAMS):
            fence(("came", q), *done, *pending, *(["tokens", "cotangent"] if step == 0 and q == 0 else []))
            done.clear()
            pending.clear()
            if t == depth - 2:
                env["came_there", q] = swap(env["came", q])
                gelu(q, i)
            elif t == depth - 1:
                receive(q, 1)
            elif i > 0:
                receive(q, t + 2)
            work = []
            if step + 1 < len(steps):
                message(q, step + 1)
                i_next, t_next = steps[step + 1]
                if t_next == depth - 2 and i_next + 1 < count:
                    work.append((forward, (q, i_next + 1), ("x", items[q][i_next + 1][0])))
                if t_next == 1 and i_next == 1 and q < HALVES:
                    work.append((transpose, (q,), ("x", q)))
                if t_next == depth - 2 and i_next > 0:
                    work.append((backward_half, (q, i_next - 1), ("got", q, depth - 1)))
                fence(("msg", q), *[name for _, _, name in work])
                start(q, step + 1)
            else:
                work.append((backward_input, (q, count - 1), None))
            if step == 1 and q == 0:
                fence("far_x", "far_y", "all", ("msg", q))
                gather_end(1)
            for piece, args, _ in work:
                piece(*args)
            if step == 0 and q == 0:
                env["cotangent_there"] = swap(env["cotangent"])
                gather_near(1)
            if step == 0 and q == STREAMS - 1:
                fence("by_x", "by_y", "all", ("msg", q))
                gather_far()
        if t == depth - 1 and i == count - 1:
            for half in range(HALVES - 1):
                scatter_input(half, False)
    scatter_input(HALVES - 1, square)
    for chunk in range(CHUNKS):
        fence(("g", HALVES - 1, chunk), ("total", HALVES - 1))
        backward_weight(chunk)

    input_grad = jnp.concatenate([input_grad[h] for h in range(HALVES)], axis=-2)
    return env["activated"], input_grad.reshape(tokens.shape), env["weight_grad"]


def solution(mesh):
    return jax.shard_map(
        on_device,
        mesh=mesh,
        in_specs=(P("col", "row"), P("row", "col"), P("row", "col")),
        out_specs=(P("row", "col"), P("col", "row"), P("row", "col")),
        check_vma=False,
    )
```

```python
import math

import jax
import jax.numpy as jnp
from jax import lax
from jax.experimental import pallas as pl
from jax.experimental.pallas import tpu as pltpu
from jax.sharding import PartitionSpec as P

BF16 = jnp.bfloat16
F32 = jnp.float32
CORES = 2
CHUNKS = 2
STREAMS = 2
HALVES = 2


def gelu_and_slope(value):
    below = 0.5 * (1.0 + lax.erf(value / math.sqrt(2.0)))
    density = jnp.exp(-0.5 * value * value) / math.sqrt(2.0 * math.pi)
    return value * below, below + value * density


def tile(extent, limit):
    best = 128
    for size in range(128, min(extent, limit) + 1, 128):
        if extent % size == 0:
            best = size
    return best


def matmul_call(body, name, grid, flops, moved, vmem=60, **spec):
    if grid is not None:
        spec["grid"] = grid
    return pl.pallas_call(
        body,
        compiler_params=pltpu.CompilerParams(vmem_limit_bytes=vmem * 2**20),
        cost_estimate=pl.CostEstimate(flops=flops, bytes_accessed=moved, transcendentals=0),
        name=name,
        **spec,
    )


def forward_matmul(x, weight, chunk, f):
    rows, width = x.shape
    bn = tile(f, 512)
    steps = f // bn

    def body(x_ref, w_ref, out):
        out[...] = jnp.dot(x_ref[...], w_ref[...], preferred_element_type=F32).astype(BF16)

    return matmul_call(
        body,
        "forward",
        (steps,),
        2 * rows * width * f,
        2 * (rows * width + width * f + rows * f),
        vmem=47,
        in_specs=[
            pl.BlockSpec((rows, width), lambda j: (0, 0)),
            pl.BlockSpec((width, bn), lambda j: (0, chunk * steps + j)),
        ],
        out_specs=pl.BlockSpec((rows, bn), lambda j: (0, j)),
        out_shape=jax.ShapeDtypeStruct((rows, f), BF16),
    )(x, weight)


def input_grad_matmul(g, weight, chunk, total, last):
    rows, f = g.shape
    width = weight.shape[0]
    bn = tile(width, 256)
    kept = [] if total is None else [total]

    def body(g_ref, w_ref, *rest):
        part = lax.dot_general(
            g_ref[...], w_ref[...], (((1,), (1,)), ((), ())), preferred_element_type=F32
        )
        if kept:
            part += rest[0][...]
        rest[-1][...] = part.astype(rest[-1].dtype)

    return matmul_call(
        body,
        "input_grad",
        (width // bn,),
        2 * rows * width * f,
        2 * (rows * f + width * f + 4 * rows * width),
        vmem=47,
        in_specs=[
            pl.BlockSpec((rows, f), lambda j: (0, 0)),
            pl.BlockSpec((bn, f), lambda j: (j, chunk)),
        ]
        + [pl.BlockSpec((rows, bn), lambda j: (0, j))] * len(kept),
        out_specs=pl.BlockSpec((rows, bn), lambda j: (0, j)),
        out_shape=jax.ShapeDtypeStruct((rows, width), BF16 if last else F32),
    )(g, weight, *kept)


def input_grad_whole(gs, weight):
    rows, f = gs[0].shape
    width, units = weight.shape
    bn = tile(width, 256)

    def body(*refs):
        g_refs, w_ref, out = refs[:-2], refs[-2], refs[-1]
        total = 0.0
        for chunk, g_ref in enumerate(g_refs):
            total += lax.dot_general(
                g_ref[...],
                w_ref[:, chunk * f : (chunk + 1) * f],
                (((1,), (1,)), ((), ())),
                preferred_element_type=F32,
            )
        out[...] = total.astype(BF16)

    return matmul_call(
        body,
        "input_grad_whole",
        (width // bn,),
        2 * rows * width * units,
        2 * (rows * units + width * units + rows * width),
        vmem=47,
        in_specs=[pl.BlockSpec((rows, f), lambda j: (0, 0))] * len(gs)
        + [pl.BlockSpec((bn, units), lambda j: (j, 0))],
        out_specs=pl.BlockSpec((rows, bn), lambda j: (0, j)),
        out_shape=jax.ShapeDtypeStruct((rows, width), BF16),
    )(*gs, weight)


def weight_grad_matmul(lefts, rights, buffer, chunk, units):
    width, rows = lefts[0].shape
    f = rights[0].shape[1]
    bn = tile(f, 512)
    steps = f // bn
    n = len(lefts)
    kept = [] if buffer is None else [buffer]

    def body(*refs):
        total = jnp.dot(refs[0][...], refs[n][...], preferred_element_type=F32)
        for i in range(1, n):
            total += jnp.dot(refs[i][...], refs[n + i][...], preferred_element_type=F32)
        refs[-1][...] = total.astype(BF16)

    return matmul_call(
        body,
        "weight_grad",
        (steps,),
        2 * n * rows * width * f,
        2 * (n * rows * width + n * rows * f + width * f),
        vmem=24,
        in_specs=[pl.BlockSpec((width, rows), lambda j: (0, 0))] * n
        + [pl.BlockSpec((rows, bn), lambda j: (0, j))] * n
        + [pl.BlockSpec(memory_space=pl.ANY)] * len(kept),
        out_specs=pl.BlockSpec((width, bn), lambda j: (0, chunk * steps + j)),
        out_shape=jax.ShapeDtypeStruct((width, units), BF16),
        input_output_aliases={2 * n: 0} if kept else {},
    )(*lefts, *rights, *kept)


def message_kernel(where, part, theirs, came, keep):
    _, cores, few, f = part.shape
    bn = tile(f, 1536)

    def body(where_ref, part_ref, theirs_ref, *rest):
        out = rest[-1]
        mine = part_ref[0].astype(F32) + theirs_ref[0].astype(F32)
        if came is not None:
            here = rest[0][...].astype(F32)
            summing = where_ref[1] > 0
            mine = jnp.where(summing, mine, here if keep else 0.0)
            if not keep:
                mine += here
        out[...] = mine.astype(BF16)

    block = pl.BlockSpec((1, cores, few, bn), lambda j, where: (where[0], 0, 0, j))
    flat = pl.BlockSpec((cores, few, bn), lambda j, where: (0, 0, j))
    given = [] if came is None else [came]
    return matmul_call(
        body,
        "message",
        None,
        0,
        0,
        vmem=8,
        grid_spec=pltpu.PrefetchScalarGridSpec(
            num_scalar_prefetch=1,
            grid=(f // bn,),
            in_specs=[block, block] + [flat] * len(given),
            out_specs=flat,
        ),
        out_shape=jax.ShapeDtypeStruct((cores, few, f), BF16),
    )(where, part, theirs, *given)


def gelu_kernel(core, part, theirs, came, came_there, cotangent, cotangent_there, half, chunk, kept):
    _, cores, few, f = part.shape
    bn = tile(f, 512)
    steps = f // bn
    kept = [] if kept is None else [kept]

    def body(core_ref, part_ref, theirs_ref, came_ref, there_ref, mine_ref, other_ref, *rest):
        slope, activated = rest[-2:]
        first = core_ref[0] == 0
        values = []
        for c in range(cores):
            pre = part_ref[0, c].astype(F32) + theirs_ref[0, c].astype(F32)
            pre = pre + came_ref[c].astype(F32) + there_ref[c].astype(F32)
            value, grad = gelu_and_slope(pre)
            values.append(value)
            mine, other = mine_ref[...].astype(F32), other_ref[...].astype(F32)
            cot = jnp.where(first == (c == 0), mine, other)
            slope[c] = (cot * grad).astype(BF16)
        activated[...] = jnp.where(first, values[0], values[1]).astype(BF16)

    block = pl.BlockSpec((1, cores, few, bn), lambda j, core: (0, 0, 0, j))
    flat = pl.BlockSpec((cores, few, bn), lambda j, core: (0, 0, j))
    rows = pl.BlockSpec((few, bn), lambda j, core: (half, chunk * steps + j))
    return matmul_call(
        body,
        "gelu",
        None,
        0,
        0,
        vmem=8,
        grid_spec=pltpu.PrefetchScalarGridSpec(
            num_scalar_prefetch=1,
            grid=(steps,),
            in_specs=[block, block, flat, flat, rows, rows]
            + [pl.BlockSpec(memory_space=pl.ANY)] * len(kept),
            out_specs=[flat, rows],
        ),
        out_shape=[
            jax.ShapeDtypeStruct((cores, few, f), BF16),
            jax.ShapeDtypeStruct(cotangent.shape, BF16),
        ],
        input_output_aliases={7: 1} if kept else {},
    )(core, part, theirs, came, came_there, cotangent, cotangent_there, *kept)


def collect_kernel(place, slope, mine, theirs, depth, vmem):
    def body(place_ref, *refs):
        slope_ref, out, sems = refs[0], refs[-2], refs[-1]
        mine_refs, their_refs = refs[1:depth], refs[depth : 2 * depth - 1]
        z, core = place_ref[0], place_ref[1]
        pltpu.make_async_copy(slope_ref, out.at[0], sems.at[0]).start()
        for j in range(1, depth):
            above = z + j < depth
            here = above == (core == 1)
            for down in (True, False):
                step = j if down else depth - j
                side = above if down else jnp.logical_not(above)

                @pl.when(side & here)
                def _():
                    pltpu.make_async_copy(mine_refs[step - 1], out.at[j], sems.at[j]).start()

                @pl.when(side & jnp.logical_not(here))
                def _():
                    pltpu.make_async_copy(their_refs[step - 1], out.at[j], sems.at[j]).start()

        for j in range(depth):
            pltpu.make_async_copy(slope_ref, out.at[j], sems.at[j]).wait()

    shape = (depth, *slope.shape)
    return matmul_call(
        body,
        "collect",
        None,
        0,
        0,
        vmem=vmem,
        grid_spec=pltpu.PrefetchScalarGridSpec(
            num_scalar_prefetch=1,
            grid=(1,),
            in_specs=[pl.BlockSpec(memory_space=pl.ANY)] * (2 * depth - 1),
            out_specs=pl.BlockSpec(shape, lambda j, place: (0, 0, 0, 0)),
            scratch_shapes=[pltpu.SemaphoreType.DMA((depth,))],
        ),
        out_shape=jax.ShapeDtypeStruct(shape, BF16),
    )(place, slope, *mine, *theirs)


def on_device(tokens, weight, cotangent):
    n_row, n_col = lax.axis_size("row"), lax.axis_size("col")
    depth = n_row // CORES
    row, col = lax.axis_index("row"), lax.axis_index("col")
    z, core = row // CORES, row % CORES
    place = jnp.where(core == 0, z, depth - 1 - z)
    width, units = weight.shape
    share = cotangent.shape[0]
    few = share // HALVES
    f = units // CHUNKS
    square = n_col == 4 and depth == 4

    def swap(value):
        return lax.ppermute(value, "row", [(r, r ^ 1) for r in range(n_row)])

    def onward(value, places):
        up = [(p * CORES, (p + 1) * CORES) for p in places]
        down = [((depth - 1 - p) * CORES + 1, (depth - 2 - p) * CORES + 1) for p in places]
        return lax.ppermute(value, "row", up + down)

    def cross(value, offset):
        return lax.ppermute(value, "col", [(c, c ^ offset) for c in range(4)])

    env = {"tokens": tokens, "cotangent": cotangent}

    def fence(*names):
        names = list(dict.fromkeys(n for n in names if n in env))
        for name, value in zip(names, lax.optimization_barrier([env[n] for n in names])):
            env[name] = value

    def gather_near(half):
        mine = env["tokens"].reshape(-1, share, width)[:, half * few : (half + 1) * few]
        env["mine"] = mine
        if square:
            env["by_x"], env["by_y"] = cross(mine, 1), cross(mine, 2)
        else:
            env["all"] = lax.all_gather(mine, "col", axis=0, tiled=True)

    def gather_far():
        if square:
            env["far_x"], env["far_y"] = cross(env["by_x"][0], 2), cross(env["by_y"][1], 1)

    def gather_end(half):
        if square:
            far = jnp.stack([env["far_x"], env["far_y"]])
            held = jnp.stack([env["mine"], env["by_x"], env["by_y"], far])
            order = [col ^ ((z + j) % depth) for j in range(depth)]
        else:
            held = env["all"].reshape(depth, CORES, few, width)
            order = [(z + j) % depth for j in range(depth)]
        blocks = [lax.dynamic_index_in_dim(held, b, 0, keepdims=False) for b in order]
        env["x", half] = jnp.concatenate(blocks).reshape(n_row * few, width)

    def columns_of(chunk):
        return slice(chunk * f, (chunk + 1) * f)

    sequence = [(half, chunk) for half in range(HALVES) for chunk in range(CHUNKS)]
    items = [sequence[q::STREAMS] for q in range(STREAMS)]
    count = len(sequence) // STREAMS
    steps = [(i, t) for i in range(count) for t in range(depth)]
    steps += [(count, t) for t in range(depth - 2)]

    input_grad, seen, done, pending = {}, {}, [], []

    def forward(q, i):
        half, chunk = items[q][i]
        part = forward_matmul(env["x", half], weight, chunk, f)
        env["part", q, i] = part.reshape(depth, CORES, few, f)
        env["theirs", q, i] = swap(env["part", q, i])
        done.append(("part", q, i))

    def transpose(half):
        env["x_t", half] = env["x", half].T
        done.append(("x_t", half))

    def backward_input(q, i):
        half, chunk = items[q][i]
        collect(q, i)
        seen["total", half] = seen.get(("total", half), 0) + 1
        last = seen["total", half] == CHUNKS
        env["total", half] = input_grad_matmul(
            env["g", half, chunk], weight, chunk, env.get(("total", half)), last
        )
        done.append(("total", half))

    def backward_half(q, i):
        collect(q, i)
        half = items[q][i][0]
        if q == STREAMS - 1:
            gs = [env["g", half, chunk] for chunk in range(CHUNKS)]
            env["total", half] = input_grad_whole(gs, weight)
            done.append(("total", half))
        else:
            done.append(("g", *items[q][i]))

    def backward_weight(chunk):
        halves = range(HALVES)
        env["weight_grad"] = weight_grad_matmul(
            [env["x_t", h] for h in halves],
            [env["g", h, chunk] for h in halves],
            env.get("weight_grad"),
            chunk,
            units,
        )

    def scatter_input(half, direct):
        pair = env["total", half].reshape(depth, CORES, few, width)
        if direct:
            blocks = []
            for offset in range(4):
                at = ((col ^ offset) + depth - z) % depth
                block = lax.dynamic_index_in_dim(pair, at, 0, keepdims=False)
                blocks.append(cross(block, offset) if offset else block)
            input_grad[half] = sum(b.astype(F32) for b in blocks).astype(BF16)
        else:
            pair = lax.dynamic_slice(
                jnp.concatenate([pair, pair]), ((depth - z) % depth, 0, 0, 0), pair.shape
            )
            total = lax.psum_scatter(
                pair.reshape(n_col, -1, few, width), "col", scatter_dimension=0, tiled=True
            )
            input_grad[half] = total.reshape(-1, few, width)

    core_there = core.astype(jnp.int32).reshape(1)
    place_there = jnp.stack([z, core]).astype(jnp.int32)

    def gelu(q, i):
        half, chunk = items[q][i]
        env["slope", q], env["activated"] = gelu_kernel(
            core_there,
            env["part", q, i],
            env["theirs", q, i],
            env["came", q],
            env["came_there", q],
            cotangent,
            env["cotangent_there"],
            half,
            chunk,
            env.get("activated"),
        )

    def collect(q, i):
        half, chunk = items[q][i]
        order = range(1, depth)
        g = collect_kernel(
            place_there,
            env["slope", q],
            [env["got", q, j] for j in order],
            [env["got_there", q, j] for j in order],
            depth,
            10 if half == 0 else 47,
        )
        env["g", half, chunk] = g.reshape(n_row * few, f)

    def message(q, step):
        i, t = steps[step]
        if t == depth - 1:
            env["msg", q] = env["slope", q]
        elif i == count:
            env["msg", q] = env["came", q]
        else:
            at = jnp.where(core == 0, depth - 1 - t, t + 1)
            env["msg", q] = message_kernel(
                jnp.stack([at, place <= t]).astype(jnp.int32),
                env["part", q, i],
                env["theirs", q, i],
                None if i == 0 and t == 0 else env["came", q],
                t == 0,
            )

    def start(q, step):
        i, t = steps[step]
        first = t + 1 if i == count else 0
        last = t + 1 if (i == 0 and t < depth - 2) else depth - 1
        env["came", q] = onward(env["msg", q], range(first, last))

    def receive(q, t):
        env["got", q, t] = env["came", q]
        env["got_there", q, t] = swap(env["came", q])
        pending.append(("got_there", q, t))

    gather_near(0)
    gather_far()
    gather_end(0)
    for q in range(STREAMS):
        forward(q, 0)
    for q in range(STREAMS):
        message(q, 0)
        fence(("msg", q), ("x", 0), "tokens", "cotangent")
        start(q, 0)
    done.clear()
    pending.clear()
    for step in range(len(steps)):
        i, t = steps[step]
        for q in range(STREAMS):
            fence(("came", q), *done, *pending, *(["tokens", "cotangent"] if step == 0 and q == 0 else []))
            done.clear()
            pending.clear()
            if t == depth - 2:
                env["came_there", q] = swap(env["came", q])
                gelu(q, i)
            elif t == depth - 1:
                receive(q, 1)
            elif i > 0:
                receive(q, t + 2)
            work = []
            if step + 1 < len(steps):
                message(q, step + 1)
                i_next, t_next = steps[step + 1]
                if t_next == depth - 2 and i_next + 1 < count:
                    work.append((forward, (q, i_next + 1), ("x", items[q][i_next + 1][0])))
                if t_next == 1 and i_next == count and q < HALVES:
                    work.append((transpose, (q,), ("x", q)))
                if t_next == depth - 2 and i_next > 0:
                    work.append((backward_half, (q, i_next - 1), ("got", q, depth - 1)))
                fence(("msg", q), *[name for _, _, name in work])
                start(q, step + 1)
            else:
                work.append((backward_input, (q, count - 1), None))
            if step == 1 and q == 0:
                fence("far_x", "far_y", "all", ("msg", q))
                gather_end(1)
            for piece, args, _ in work:
                piece(*args)
            if step == 0 and q == 0:
                env["cotangent_there"] = swap(env["cotangent"])
                gather_near(1)
            if step == 0 and q == STREAMS - 1:
                fence("by_x", "by_y", "all", ("msg", q))
                gather_far()
        if t == depth - 1 and i == count - 1:
            for half in range(HALVES - 1):
                scatter_input(half, False)
    scatter_input(HALVES - 1, square)
    for chunk in range(CHUNKS):
        fence(("g", HALVES - 1, chunk), ("total", HALVES - 1))
        backward_weight(chunk)

    input_grad = jnp.concatenate([input_grad[h] for h in range(HALVES)], axis=-2)
    return env["activated"], input_grad.reshape(tokens.shape), env["weight_grad"]


def solution(mesh):
    return jax.shard_map(
        on_device,
        mesh=mesh,
        in_specs=(P("col", "row"), P("row", "col"), P("row", "col")),
        out_specs=(P("row", "col"), P("col", "row"), P("row", "col")),
        check_vma=False,
    )
```
